768 devices in a mesh: inter: 128 (over z_hi, x, y), intra: 6 (over z_lo, core).
Axes of the slice: x: 4, y: 8, z: 12 (z_hi: 4, z_lo: 3; z = z_hi * 3 + z_lo), core: 2. Of those that a mesh axis runs over, the one named last changes fastest.
Arguments:
- grad_out: bfloat16 [393216, 1536], P(('inter', 'intra')), may hold values from -24 to 24
- context: bfloat16 [393216, 768], P(('inter', 'intra')), may hold values from -6 to 6
- codes: bfloat16 [6, 256, 768], P('intra'), may hold values from -127 to 127, as said below
- scales: bfloat16 [6, 768], P('intra'), may hold values from 9.9658966e-05 to 0.0009994507
Outputs:
- ctx_grad: bfloat16 [393216, 768], P(('inter', 'intra'))
- weight_grad: float32 [1536, 768], P(('inter', 'intra'))
- bias_grad: float32 [1536], P(('inter', 'intra'))
The draws below stay inside these ranges and needn't reach their ends.
Inputs may be any that keep to these rules, and one draw needn't show every extreme that they name: codes are whole numbers.
All inputs are finite; a program needn't handle non-finite values.
Results may differ from the reference program's by a relative error of at most 0.0049.
Values may be sent and summed in bfloat16 or wider, within the bound.
No kernel may reach another device: no remote copies, remote signals or barrier semaphores. Data moves between devices by JAX's collectives and lax.ppermute only.
A program may use at most 64 MiB of HBM per device.

```python
import math
import jax
import jax.numpy as jnp
from jax import lax

D = 1536
HEAD_DIM = 96
HEADS = 8
BLOCK = 256
TOK_DEV = 512
TOKENS = 393216
N_INTER = 128
N_INTRA = 6


def draw_codes(key, part):
    key = jax.random.fold_in(key, 7)
    shape = (D // BLOCK, BLOCK, HEADS * HEAD_DIM)
    values = jax.random.randint(key, shape, -127, 128)
    along_block = lax.broadcasted_iota(jnp.int32, shape, 1)
    along_column = lax.broadcasted_iota(jnp.int32, shape, 2)
    values = jnp.where((along_block == 0) & (along_column == 0), 127, values)
    values = jnp.where((along_block == 1) & (along_column == 0), -127, values)
    return values.astype(jnp.float32).astype(jnp.bfloat16)


def spiked(drawn, key, source, target, parts, factor):
    def block_of(dim):
        return (jnp.arange(drawn.shape[dim]) // (drawn.shape[dim] // parts)).reshape((-1,) + (1,) * (drawn.ndim - 1 - dim))

    near = jax.random.permutation(key, parts)[block_of(target)]
    other_side = (block_of(target) + parts // 2) % parts
    return jnp.where((block_of(source) == near) | (block_of(source) == other_side), factor * drawn, drawn)


def shard_levels(stream_key, extent, split, smallest, top_value):
    gain, own = 1.0, jax.random.fold_in(stream_key, 6)
    for position, blocks in split:
        heights = jnp.exp(jax.random.uniform(jax.random.fold_in(own, position), (blocks,), jnp.float32, smallest / len(split), top_value / len(split)))
        gain = gain * jnp.repeat(heights, extent[position] // blocks).reshape([-1 if axis == position else 1 for axis in range(len(extent))])
    return gain


def centred(key, shape, width, reach, shards=(), kind=jnp.bfloat16):
    level = shard_levels(key, shape, shards, -0.22, 0.18) if shards else 1.0
    result = jax.random.normal(key, shape, jnp.float32) * width * level
    return jnp.minimum(jnp.maximum(result, -reach), reach).astype(kind)


def gaussian_with(key, extent, scale, limit, split, heavy, held_as=jnp.bfloat16):
    entries = scale * jax.random.normal(key, extent, jnp.float32)
    if split:
        entries = entries * shard_levels(key, extent, split, -0.22, 0.18)
    return jnp.clip(spiked(entries, jax.random.fold_in(key, 3), *heavy), -limit, limit).astype(held_as)


def setup_inputs(seed: int = 0) -> dict:
    key_of = jax.random.split(jax.random.key(seed), 5)
    grad_out = gaussian_with(key_of[0], (TOKENS, D), 1.0, 24.0, ((0, 768),), (0, 1, 768, 6.0))
    context = centred(key_of[1], (TOKENS, HEADS * HEAD_DIM), 1.0, 6.0, ((0, 768),))
    codes = draw_codes(jax.random.fold_in(key_of[4], 71), 0)
    scales = jnp.clip(jnp.exp(math.log(0.0009994507) - 2.3054518 * jax.random.uniform(key_of[3], (D // BLOCK, HEADS * HEAD_DIM), jnp.float32) ** shard_levels(key_of[3], (D // BLOCK, HEADS * HEAD_DIM), ((0, 6),), -0.2, 0.2)), 9.965896606445312e-05, 0.0009994507).astype(jnp.bfloat16)
    return dict(grad_out=grad_out, context=context, codes=codes, scales=scales)


def reference(grad_out, context, codes, scales):
    heads_width = HEADS * HEAD_DIM
    weight = (codes.astype(jnp.float32) * scales[:, None, :].astype(jnp.float32)).astype(jnp.bfloat16)
    weight_wide = weight.reshape(D, heads_width).astype(jnp.float32)
    device_count = N_INTER * N_INTRA
    average = 1.0 / device_count
    token_blocks = grad_out.reshape(device_count, TOK_DEV, D)
    context_blocks = context.reshape(device_count, TOK_DEV, heads_width)

    def accumulate(running, device_slice):
        outgoing, saved_ctx = device_slice
        outgoing = outgoing.astype(jnp.float32)
        saved_ctx = saved_ctx.astype(jnp.float32)
        ctx_piece = jnp.dot(outgoing, weight_wide, precision=lax.Precision.HIGHEST, preferred_element_type=jnp.float32).astype(jnp.bfloat16)
        local_term = jnp.dot(outgoing.T, saved_ctx, precision=lax.Precision.HIGHEST, preferred_element_type=jnp.float32) * average
        local_bias = jnp.sum(outgoing, axis=0) * average
        return (running[0] + local_term, running[1] + local_bias), ctx_piece

    initial = (jnp.zeros((D, heads_width), jnp.float32), jnp.zeros((D,), jnp.float32))
    sums, ctx_blocks = lax.scan(accumulate, initial, (token_blocks, context_blocks))
    return ctx_blocks.reshape(TOKENS, heads_width), sums[0], sums[1]
```

```python
import functools
import jax
import jax.numpy as jnp
import numpy as np
from jax import lax
from jax.experimental import pallas as pl
from jax.experimental.pallas import tpu as pltpu
from jax.sharding import Mesh, PartitionSpec as P

SIZES = (4, 4, 4, 2, 3, 2)
NAMES = ("zh", "x", "yh", "yl", "zl", "c")
PAD = 128


def row_map(sizes):
    _, x, yh, yl, zl, _ = sizes
    index = np.arange(2 * x * yh * yl * zl * 4).reshape(2, x, yh, yl, zl, 2, 2)[..., :1, :]
    one = np.transpose(index, (5, 6, 1, 3, 0, 2, 4)).reshape(-1)
    return np.concatenate([one, one]).astype(np.int32)[:, None]


def split_pairs(values):
    lane = lax.broadcasted_iota(jnp.int32, (values[0].shape[0], PAD), 1)
    parts = jnp.zeros(lane.shape, jnp.float32)
    for s, value in enumerate(values):
        high = value.astype(jnp.bfloat16).astype(jnp.float32)
        parts = jnp.where(lane == 2 * s, high, parts)
        parts = jnp.where(lane == 2 * s + 1, value - high, parts)
    return parts


def join_pairs(parts):
    lane = lax.broadcasted_iota(jnp.int32, parts.shape, 1)
    return [
        jnp.sum(jnp.where((lane == 2 * s) | (lane == 2 * s + 1), parts, 0.0), axis=1, keepdims=True)
        for s in range(2)
    ]


def term_kernel(map_hbm, grad_hbm, ctx_hbm, codes_hbm, scales_hbm, send_ref, keep_ref, weight_ref, *scratch):
    map_ref, grad_ref, ctx_ref, codes_ref, scales_ref, acc, sems = scratch
    core = lax.axis_index("c")
    span = map_ref.shape[0]
    half = span // 2
    width = ctx_ref.shape[1]
    tokens = ctx_ref.shape[0]
    blocks = send_ref.shape[0]
    part = send_ref.shape[1] // 2

    def columns(step):
        return pl.ds(step * span, span)

    copies = [
        pltpu.make_async_copy(map_hbm, map_ref, sems.at[0]),
        pltpu.make_async_copy(grad_hbm.at[:, columns(0)], grad_ref.at[:, columns(0)], sems.at[1]),
        pltpu.make_async_copy(ctx_hbm, ctx_ref, sems.at[2]),
        pltpu.make_async_copy(grad_hbm.at[:, columns(1)], grad_ref.at[:, columns(1)], sems.at[3]),
        pltpu.make_async_copy(scales_hbm, scales_ref, sems.at[4]),
        pltpu.make_async_copy(codes_hbm, codes_ref, sems.at[5]),
    ]
    for copy in copies:
        copy.start()
    copies[0].wait()
    row = lax.broadcasted_iota(jnp.int32, (span, 1), 0)
    other = jnp.where(row < half, 1 - core, core)
    source = map_ref[...] + 2 * other
    column = lax.broadcasted_iota(jnp.int32, (span, span), 1)
    pick = jnp.where(source == column, 1.0, 0.0).astype(jnp.bfloat16)
    ones = jnp.ones((tokens, PAD), jnp.bfloat16)
    for step in range(2):
        copies[1 + 2 * step].wait()
        moved = lax.dot_general(
            pick,
            grad_ref[:, step * span : (step + 1) * span],
            (((1,), (1,)), ((), ())),
            preferred_element_type=jnp.float32,
        ).astype(jnp.bfloat16)
        if step == 0:
            copies[2].wait()
        acc[step, :, :width] = jnp.dot(moved, ctx_ref[...], preferred_element_type=jnp.float32)
        acc[step, :, width:] = jnp.dot(moved, ones, preferred_element_type=jnp.float32)
    copies[4].wait()
    copies[5].wait()
    scaled = codes_ref[0].astype(jnp.float32) * scales_ref[...].astype(jnp.float32)
    weight_ref[...] = scaled.astype(jnp.bfloat16)
    for side, out in enumerate((send_ref, keep_ref)):
        for block in range(blocks):
            sums = []
            for s in range(2):
                at = ((side * 2 + s) * blocks + block) * part
                rows = jnp.concatenate([acc[0, at : at + part, :], acc[1, at : at + part, :]], axis=0)
                out[block, :, s * width : (s + 1) * width] = rows[:, :width].astype(jnp.bfloat16)
                sums.append(rows[:, width:])
            out[block, :, 2 * width :] = split_pairs(sums).astype(jnp.bfloat16)


def local_terms(sizes, grad_out, context, codes, scales):
    zh, x, yh, yl, zl, _ = sizes
    width = context.shape[1]
    piece = jax.ShapeDtypeStruct((x * yl, zh * yh * zl, 2 * width + PAD), jnp.bfloat16)
    block = jax.ShapeDtypeStruct(codes.shape[1:], jnp.bfloat16)
    rows = row_map(sizes)
    operands = (jnp.asarray(rows), grad_out, context, codes, scales)
    return pl.pallas_call(
        term_kernel,
        out_shape=(piece, piece, block),
        in_specs=[pl.BlockSpec(memory_space=pltpu.HBM)] * 5,
        out_specs=(pl.BlockSpec(memory_space=pltpu.VMEM),) * 3,
        scratch_shapes=[pltpu.VMEM(a.shape, a.dtype) for a in operands]
        + [pltpu.VMEM((2, rows.shape[0], width + PAD), jnp.float32), pltpu.SemaphoreType.DMA((6,))],
        compiler_params=pltpu.CompilerParams(vmem_limit_bytes=60 * 1024 * 1024),
        cost_estimate=pl.CostEstimate(flops=4 * 10**9, bytes_accessed=5 * 10**6, transcendentals=0),
    )(*operands)


def chip_kernel(got_ref, keep_ref, out_ref):
    wide = out_ref.shape[2] - PAD
    for block in range(out_ref.shape[0]):
        total = got_ref[block].astype(jnp.float32) + keep_ref[block].astype(jnp.float32)
        out_ref[block, :, :wide] = total[:, :wide].astype(out_ref.dtype)
        out_ref[block, :, wide:] = split_pairs(join_pairs(total[:, wide:])).astype(out_ref.dtype)


def chip_sum(got, keep):
    whole = pl.BlockSpec(memory_space=pltpu.VMEM)
    return pl.pallas_call(
        chip_kernel,
        out_shape=jax.ShapeDtypeStruct(got.shape, got.dtype),
        in_specs=[whole] * 2,
        out_specs=whole,
        compiler_params=pltpu.CompilerParams(vmem_limit_bytes=16 * 1024 * 1024),
        cost_estimate=pl.CostEstimate(flops=10**6, bytes_accessed=4 * 10**6, transcendentals=0),
    )(got, keep)


def near_kernel(got_ref, *refs):
    held, (sum_ref, own_ref, wide) = refs[:-3], refs[-3:]
    rows = held[0].shape[0]
    for index, block in enumerate(held):
        own_ref[index * rows : (index + 1) * rows, :] = block[...]
    for chunk in range(sum_ref.shape[1]):
        lanes = slice(chunk * PAD, (chunk + 1) * PAD)
        total = got_ref[0, :, lanes].astype(jnp.float32)
        for index in range(1, got_ref.shape[0]):
            total = total + got_ref[index, :, lanes].astype(jnp.float32)
        if chunk == sum_ref.shape[1] - 1:
            total = split_pairs(join_pairs(total))
        wide[:, chunk, :] = total
    sum_ref[...] = wide[...].astype(sum_ref.dtype)


def near_sum(got, held):
    _, rows, lanes = got.shape
    shape = (rows, lanes // PAD, PAD)
    tall = (len(held) * held[0].shape[0], held[0].shape[1])
    whole = pl.BlockSpec(memory_space=pltpu.VMEM)
    return pl.pallas_call(
        near_kernel,
        out_shape=(jax.ShapeDtypeStruct(shape, jnp.bfloat16), jax.ShapeDtypeStruct(tall, jnp.bfloat16)),
        in_specs=[whole] * (1 + len(held)),
        out_specs=(whole, whole),
        scratch_shapes=[pltpu.VMEM(shape, jnp.float32)],
        compiler_params=pltpu.CompilerParams(vmem_limit_bytes=24 * 1024 * 1024),
        cost_estimate=pl.CostEstimate(flops=10**6, bytes_accessed=4 * 10**6, transcendentals=0),
    )(got, *held)


def last_kernel(scale, far_ref, weight_ref, bias_ref):
    total = far_ref[0].astype(jnp.float32)
    for index in range(1, far_ref.shape[0]):
        total = total + far_ref[index].astype(jnp.float32)
    total = total * scale
    chunks = (total.shape[0] - 1) // 2
    for s in range(2):
        for chunk in range(chunks):
            at = s * chunks + chunk
            weight_ref[s : s + 1, chunk * PAD : (chunk + 1) * PAD] = total[at : at + 1, :]
    tail = total[2 * chunks : 2 * chunks + 1, :]
    lane = lax.broadcasted_iota(jnp.int32, (1, PAD), 1)
    for s in range(2):
        bias_ref[s] = jnp.sum(jnp.where((lane == 2 * s) | (lane == 2 * s + 1), tail, 0.0))


def last_sum(far, scale):
    width = (far.shape[1] - 1) // 2 * PAD
    whole = pl.BlockSpec(memory_space=pltpu.VMEM)
    return pl.pallas_call(
        functools.partial(last_kernel, scale),
        out_shape=(jax.ShapeDtypeStruct((2, width), jnp.float32), jax.ShapeDtypeStruct((2,), jnp.float32)),
        in_specs=[whole],
        out_specs=(pl.BlockSpec((2, width), lambda: (0, 0)), pl.BlockSpec(memory_space=pltpu.SMEM)),
        compiler_params=pltpu.CompilerParams(vmem_limit_bytes=16 * 1024 * 1024),
        cost_estimate=pl.CostEstimate(flops=10**5, bytes_accessed=2 * 10**5, transcendentals=0),
    )(far)


def ctx_kernel(chips, grad_ref, own_ref, sibling_ref, out_ref):
    chip, core = lax.axis_index("zl"), lax.axis_index("c")
    rows = own_ref.shape[0] // chips
    total = None
    for back in range(chips):
        owner = lax.rem(chip + chips - back, chips)
        for held, side in ((own_ref, core), (sibling_ref, 1 - core)):
            at = pl.multiple_of((2 * owner + side) * rows, rows)
            product = jnp.dot(
                grad_ref[:, pl.ds(at, rows)],
                held[back * rows : (back + 1) * rows, :],
                preferred_element_type=jnp.float32,
            )
            total = product if total is None else total + product
    out_ref[...] = total.astype(out_ref.dtype)


def ctx_product(chips, grad_out, own, sibling):
    tokens, depth = grad_out.shape
    steps = 2
    whole = pl.BlockSpec(memory_space=pltpu.VMEM)
    return pl.pallas_call(
        functools.partial(ctx_kernel, chips),
        out_shape=jax.ShapeDtypeStruct((tokens, own.shape[1]), jnp.bfloat16),
        grid=(steps,),
        in_specs=[pl.BlockSpec((tokens // steps, depth), lambda i: (i, 0)), whole, whole],
        out_specs=pl.BlockSpec((tokens // steps, own.shape[1]), lambda i: (i, 0)),
        compiler_params=pltpu.CompilerParams(vmem_limit_bytes=24 * 1024 * 1024),
        cost_estimate=pl.CostEstimate(flops=12 * 10**8, bytes_accessed=5 * 10**6, transcendentals=0),
    )(grad_out, own, sibling)


def body(sizes, grad_out, context, codes, scales):
    count = int(np.prod(sizes))
    chips = sizes[4]
    swap = [(0, 1), (1, 0)]

    send, keep, block = local_terms(sizes, grad_out, context, codes, scales)
    got = lax.ppermute(send, "c", swap)
    held = [block]
    for shift in range(1, chips):
        held.append(lax.ppermute(block, "zl", [(i, (i + shift) % chips) for i in range(chips)]))

    chip = chip_sum(got, keep)
    near = lax.all_to_all(chip, ("x", "yl"), split_axis=0, concat_axis=0, tiled=True)
    near, own = near_sum(near, held)
    sibling = lax.ppermute(own, "c", swap)
    far = lax.all_to_all(near, ("zh", "yh", "zl"), split_axis=0, concat_axis=0, tiled=True)
    weight_grad, bias_grad = last_sum(far, 1.0 / count)

    ctx_grad = ctx_product(chips, grad_out, own, sibling)
    return ctx_grad, weight_grad, bias_grad


def solution(mesh, sizes=SIZES):
    fine = Mesh(mesh.devices.reshape(sizes), NAMES)
    in_specs = (P(NAMES, None), P(NAMES, None), P(("zl", "c"), None, None), P(("zl", "c"), None))
    out_specs = (P(NAMES, None), P(NAMES, None), P(NAMES))
    return jax.shard_map(
        functools.partial(body, sizes), mesh=fine, in_specs=in_specs, out_specs=out_specs, check_vma=False
    )
```

```python
import functools
import jax
import jax.numpy as jnp
import numpy as np
from jax import lax
from jax.experimental import pallas as pl
from jax.experimental.pallas import tpu as pltpu
from jax.sharding import Mesh, PartitionSpec as P

SIZES = (4, 4, 4, 2, 3, 2)
NAMES = ("zh", "x", "yh", "yl", "zl", "c")
PAD = 128


ANY = pl.BlockSpec(memory_space=pl.ANY)
VMEM = pl.BlockSpec(memory_space=pltpu.VMEM)


def parameters():
    return pltpu.CompilerParams(vmem_limit_bytes=64 * 1024 * 1024)


def row_map(sizes):
    _, x, yh, yl, zl, _ = sizes
    index = np.arange(2 * x * yh * yl * zl * 4).reshape(2, x, yh, yl, zl, 2, 2)[..., :1, :]
    return np.transpose(index, (5, 6, 1, 3, 2, 0, 4)).reshape(-1, 1).astype(np.int32)


def split_pairs(values):
    lane = lax.broadcasted_iota(jnp.int32, (values[0].shape[0], PAD), 1)
    parts = jnp.zeros(lane.shape, jnp.float32)
    for s, value in enumerate(values):
        high = value.astype(jnp.bfloat16).astype(jnp.float32)
        parts = jnp.where(lane == 2 * s, high, parts)
        parts = jnp.where(lane == 2 * s + 1, value - high, parts)
    return parts


def join_pairs(parts):
    lane = lax.broadcasted_iota(jnp.int32, parts.shape, 1)
    return [
        jnp.sum(jnp.where((lane == 2 * s) | (lane == 2 * s + 1), parts, 0.0), axis=1, keepdims=True)
        for s in range(2)
    ]


def term_kernel(mine, *refs):
    count = 5 if mine else 3
    inputs, refs = refs[:count], refs[count:]
    outputs, refs = refs[: 1 + mine], refs[1 + mine :]
    held, (acc, done, in_sems, out_sems) = refs[:count], refs[count:]
    map_ref, grad_ref, ctx_ref = held[:3]
    core = lax.axis_index("c")
    rows = map_ref.shape[0]
    span = 2 * rows
    width = ctx_ref.shape[1]
    blocks, part = done.shape[0], done.shape[1] // 2

    def columns(step):
        return pl.ds(step * span, span)

    copies = [
        pltpu.make_async_copy(inputs[1].at[:, columns(0)], grad_ref.at[:, columns(0)], in_sems.at[0]),
        pltpu.make_async_copy(inputs[0], map_ref, in_sems.at[1]),
        pltpu.make_async_copy(inputs[2], ctx_ref, in_sems.at[2]),
        pltpu.make_async_copy(inputs[1].at[:, columns(1)], grad_ref.at[:, columns(1)], in_sems.at[3]),
    ]
    for extra in range(3, count):
        copies.append(pltpu.make_async_copy(inputs[extra], held[extra], in_sems.at[extra + 1]))
    for copy in copies:
        copy.start()
    copies[1].wait()
    source = map_ref[...] + 2 * (core if mine else 1 - core)
    column = lax.broadcasted_iota(jnp.int32, (rows, span), 1)
    pick = jnp.where(source == column, 1.0, 0.0).astype(jnp.bfloat16)
    ones = jnp.ones((ctx_ref.shape[0], PAD), jnp.bfloat16)
    for step in range(2):
        copies[3 * step].wait()
        moved = lax.dot_general(
            pick,
            grad_ref[:, step * span : (step + 1) * span],
            (((1,), (1,)), ((), ())),
            preferred_element_type=jnp.float32,
        ).astype(jnp.bfloat16)
        if step == 0:
            copies[2].wait()
        acc[step, :, :width] = jnp.dot(moved, ctx_ref[...], preferred_element_type=jnp.float32)
        acc[step, :, width:] = jnp.dot(moved, ones, preferred_element_type=jnp.float32)
    sent = []
    for block in range(blocks):
        sums = []
        for s in range(2):
            at = (s * blocks + block) * part
            both = jnp.concatenate([acc[0, at : at + part, :], acc[1, at : at + part, :]], axis=0)
            done[block, :, s * width : (s + 1) * width] = both[:, :width].astype(jnp.bfloat16)
            sums.append(both[:, width:])
        done[block, :, 2 * width :] = split_pairs(sums).astype(jnp.bfloat16)
        sent.append(pltpu.make_async_copy(done.at[block], outputs[0].at[block], out_sems.at[block]))
        sent[-1].start()
    if mine:
        copies[4].wait()
        copies[5].wait()
        scaled = held[3][0].astype(jnp.float32) * held[4][...].astype(jnp.float32)
        outputs[1][...] = scaled.astype(jnp.bfloat16)
    for copy in sent:
        copy.wait()


def local_terms(sizes, mine, grad_out, context, *weights):
    zh, x, yh, yl, zl, _ = sizes
    width = context.shape[1]
    piece = jax.ShapeDtypeStruct((x * yl, zh * yh * zl, 2 * width + PAD), jnp.bfloat16)
    rows = row_map(sizes)
    operands = (jnp.asarray(rows), grad_out, context, *weights)
    shapes, specs = (piece,), (ANY,)
    if mine:
        shapes += (jax.ShapeDtypeStruct(weights[0].shape[1:], jnp.bfloat16),)
        specs += (VMEM,)
    return pl.pallas_call(
        functools.partial(term_kernel, mine),
        out_shape=shapes,
        in_specs=[ANY] * len(operands),
        out_specs=specs,
        scratch_shapes=[pltpu.VMEM(a.shape, a.dtype) for a in operands]
        + [
            pltpu.VMEM((2, rows.shape[0], width + PAD), jnp.float32),
            pltpu.VMEM(piece.shape, piece.dtype),
            pltpu.SemaphoreType.DMA((6,)),
            pltpu.SemaphoreType.DMA((piece.shape[0],)),
        ],
        compiler_params=parameters(),
        cost_estimate=pl.CostEstimate(flops=2 * 10**9, bytes_accessed=5 * 10**6, transcendentals=0),
    )(*operands)


def ctx_kernel(chips, grad_hbm, own_hbm, sibling_hbm, out_hbm, grad_ref, weight_ref, out_ref, in_sems, out_sems):
    chip, core = lax.axis_index("zl"), lax.axis_index("c")
    rows = own_hbm.shape[0] // chips
    half = grad_hbm.shape[0] // 2

    def tokens(step):
        return pl.ds(step * half, half)

    grads = [
        pltpu.make_async_copy(grad_hbm.at[tokens(i)], grad_ref.at[tokens(i)], in_sems.at[i]) for i in range(2)
    ]
    blocks = []
    for side, held in enumerate((own_hbm, sibling_hbm)):
        for back in range(chips):
            slot = side * chips + back
            blocks.append(
                pltpu.make_async_copy(
                    held.at[pl.ds(back * rows, rows)],
                    weight_ref.at[pl.ds(slot * rows, rows)],
                    in_sems.at[2 + slot],
                )
            )
    grads[0].start()
    for copy in blocks:
        copy.start()
    grads[1].start()
    outs = []
    for step in range(2):
        grads[step].wait()
        total = None
        for slot in range(2 * chips):
            if step == 0:
                blocks[slot].wait()
            owner = lax.rem(chip + chips - slot % chips, chips)
            side = core if slot < chips else 1 - core
            at = pl.multiple_of((2 * owner + side) * rows, rows)
            product = jnp.dot(
                grad_ref[step * half : (step + 1) * half, pl.ds(at, rows)],
                weight_ref[slot * rows : (slot + 1) * rows, :],
                preferred_element_type=jnp.float32,
            )
            total = product if total is None else total + product
        out_ref[step * half : (step + 1) * half, :] = total.astype(out_ref.dtype)
        outs.append(pltpu.make_async_copy(out_ref.at[tokens(step)], out_hbm.at[tokens(step)], out_sems.at[step]))
        outs[-1].start()
    for copy in outs:
        copy.wait()


def ctx_product(chips, grad_out, own, sibling):
    out = jax.ShapeDtypeStruct((grad_out.shape[0], own.shape[1]), jnp.bfloat16)
    return pl.pallas_call(
        functools.partial(ctx_kernel, chips),
        out_shape=out,
        in_specs=[ANY] * 3,
        out_specs=ANY,
        scratch_shapes=[
            pltpu.VMEM(grad_out.shape, grad_out.dtype),
            pltpu.VMEM((2 * own.shape[0], own.shape[1]), own.dtype),
            pltpu.VMEM(out.shape, out.dtype),
            pltpu.SemaphoreType.DMA((2 + 2 * chips,)),
            pltpu.SemaphoreType.DMA((2,)),
        ],
        compiler_params=parameters(),
        cost_estimate=pl.CostEstimate(flops=12 * 10**8, bytes_accessed=5 * 10**6, transcendentals=0),
    )(grad_out, own, sibling)


def chip_kernel(got_hbm, keep_hbm, out_hbm, got_ref, keep_ref, out_ref, in_sems, out_sems):
    wide = out_ref.shape[2] - PAD
    blocks = range(out_ref.shape[0])
    pairs = []
    for b in blocks:
        pairs.append(
            (
                pltpu.make_async_copy(got_hbm.at[b], got_ref.at[b], in_sems.at[0, b]),
                pltpu.make_async_copy(keep_hbm.at[b], keep_ref.at[b], in_sems.at[1, b]),
            )
        )
        for copy in pairs[-1]:
            copy.start()
    outs = []
    for b in blocks:
        for copy in pairs[b]:
            copy.wait()
        total = got_ref[b].astype(jnp.float32) + keep_ref[b].astype(jnp.float32)
        out_ref[b, :, :wide] = total[:, :wide].astype(out_ref.dtype)
        out_ref[b, :, wide:] = split_pairs(join_pairs(total[:, wide:])).astype(out_ref.dtype)
        outs.append(pltpu.make_async_copy(out_ref.at[b], out_hbm.at[b], out_sems.at[b]))
        outs[-1].start()
    for copy in outs:
        copy.wait()


def chip_sum(got, keep):
    return pl.pallas_call(
        chip_kernel,
        out_shape=jax.ShapeDtypeStruct(got.shape, got.dtype),
        in_specs=[ANY] * 2,
        out_specs=ANY,
        scratch_shapes=[pltpu.VMEM(got.shape, got.dtype)] * 3
        + [pltpu.SemaphoreType.DMA((2, got.shape[0])), pltpu.SemaphoreType.DMA((got.shape[0],))],
        compiler_params=parameters(),
        cost_estimate=pl.CostEstimate(flops=10**6, bytes_accessed=4 * 10**6, transcendentals=0),
    )(got, keep)


def near_kernel(groups, got_hbm, sum_ref, got_ref, wide, sems):
    copies = [
        pltpu.make_async_copy(got_hbm.at[b], got_ref.at[b], sems.at[b]) for b in range(got_ref.shape[0])
    ]
    for copy in copies:
        copy.start()
    for copy in copies:
        copy.wait()
    for chunk in range(sum_ref.shape[1]):
        lanes = slice(chunk * PAD, (chunk + 1) * PAD)
        total = got_ref[0, :, lanes].astype(jnp.float32)
        for index in range(1, got_ref.shape[0]):
            total = total + got_ref[index, :, lanes].astype(jnp.float32)
        if chunk == sum_ref.shape[1] - 1:
            total = split_pairs(join_pairs(total))
        wide[:, chunk, :] = total
    rest = sum_ref.shape[0] // (2 * groups)
    for high in range(2):
        for group in range(groups):
            to, at = (2 * group + high) * rest, (high * groups + group) * rest
            sum_ref[to : to + rest] = wide[at : at + rest].astype(sum_ref.dtype)


def near_sum(groups, got):
    _, rows, lanes = got.shape
    shape = (rows, lanes // PAD, PAD)
    return pl.pallas_call(
        functools.partial(near_kernel, groups),
        out_shape=jax.ShapeDtypeStruct(shape, jnp.bfloat16),
        in_specs=[ANY],
        out_specs=VMEM,
        scratch_shapes=[
            pltpu.VMEM(got.shape, got.dtype),
            pltpu.VMEM(shape, jnp.float32),
            pltpu.SemaphoreType.DMA((got.shape[0],)),
        ],
        compiler_params=parameters(),
        cost_estimate=pl.CostEstimate(flops=10**6, bytes_accessed=15 * 10**5, transcendentals=0),
    )(got)


def middle_kernel(got_ref, *refs):
    held, (sum_ref, own_hbm, wide, sems) = refs[:-4], refs[-4:]
    rows = held[0].shape[0]
    copies = [
        pltpu.make_async_copy(block, own_hbm.at[pl.ds(i * rows, rows)], sems.at[i]) for i, block in enumerate(held)
    ]
    for copy in copies:
        copy.start()
    many = sum_ref.shape[0]
    total = got_ref[0:many].astype(jnp.float32)
    for index in range(1, got_ref.shape[0] // many):
        total = total + got_ref[index * many : (index + 1) * many].astype(jnp.float32)
    wide[...] = total
    last = wide.shape[1] - 1
    wide[:, last, :] = split_pairs(join_pairs(wide[:, last, :]))
    sum_ref[...] = wide[...].astype(sum_ref.dtype)
    for copy in copies:
        copy.wait()


def middle_sum(groups, got, held):
    shape = (got.shape[0] // groups, *got.shape[1:])
    tall = (len(held) * held[0].shape[0], held[0].shape[1])
    return pl.pallas_call(
        middle_kernel,
        out_shape=(jax.ShapeDtypeStruct(shape, jnp.bfloat16), jax.ShapeDtypeStruct(tall, jnp.bfloat16)),
        in_specs=[VMEM] + [ANY] * len(held),
        out_specs=(VMEM, ANY),
        scratch_shapes=[pltpu.VMEM(shape, jnp.float32), pltpu.SemaphoreType.DMA((len(held),))],
        compiler_params=parameters(),
        cost_estimate=pl.CostEstimate(flops=10**6, bytes_accessed=3 * 10**6, transcendentals=0),
    )(got, *held)


def last_kernel(scale, far_ref, weight_ref, bias_ref):
    total = far_ref[0].astype(jnp.float32)
    for index in range(1, far_ref.shape[0]):
        total = total + far_ref[index].astype(jnp.float32)
    total = total * scale
    chunks = (total.shape[0] - 1) // 2
    for s in range(2):
        for chunk in range(chunks):
            at = s * chunks + chunk
            weight_ref[s : s + 1, chunk * PAD : (chunk + 1) * PAD] = total[at : at + 1, :]
    tail = total[2 * chunks : 2 * chunks + 1, :]
    lane = lax.broadcasted_iota(jnp.int32, (1, PAD), 1)
    for s in range(2):
        bias_ref[s] = jnp.sum(jnp.where((lane == 2 * s) | (lane == 2 * s + 1), tail, 0.0))


def last_sum(far, scale):
    width = (far.shape[1] - 1) // 2 * PAD
    return pl.pallas_call(
        functools.partial(last_kernel, scale),
        out_shape=(jax.ShapeDtypeStruct((2, width), jnp.float32), jax.ShapeDtypeStruct((2,), jnp.float32)),
        in_specs=[VMEM],
        out_specs=(pl.BlockSpec((2, width), lambda: (0, 0)), pl.BlockSpec(memory_space=pltpu.SMEM)),
        compiler_params=parameters(),
        cost_estimate=pl.CostEstimate(flops=10**5, bytes_accessed=2 * 10**5, transcendentals=0),
    )(far)


def body(sizes, grad_out, context, codes, scales):
    count = int(np.prod(sizes))
    chips = sizes[4]
    swap = [(0, 1), (1, 0)]

    (send,) = local_terms(sizes, False, grad_out, context)
    got = lax.ppermute(send, "c", swap)
    keep, block = local_terms(sizes, True, grad_out, context, codes, scales)
    held = [block]
    for shift in range(1, chips):
        held.append(lax.ppermute(block, "zl", [(i, (i + shift) % chips) for i in range(chips)]))

    near = lax.all_to_all(chip_sum(got, keep), ("x", "yl"), split_axis=0, concat_axis=0, tiled=True)
    near = near_sum(sizes[2], near)
    middle = lax.all_to_all(near, "yh", split_axis=0, concat_axis=0, tiled=True)
    middle, own = middle_sum(sizes[2], middle, held)
    sibling = lax.ppermute(own, "c", swap)
    far = lax.all_to_all(middle, ("zh", "zl"), split_axis=0, concat_axis=0, tiled=True)
    weight_grad, bias_grad = last_sum(far, 1.0 / count)

    ctx_grad = ctx_product(chips, grad_out, own, sibling)
    return ctx_grad, weight_grad, bias_grad


def solution(mesh, sizes=SIZES):
    fine = Mesh(mesh.devices.reshape(sizes), NAMES)
    in_specs = (P(NAMES, None), P(NAMES, None), P(("zl", "c"), None, None), P(("zl", "c"), None))
    out_specs = (P(NAMES, None), P(NAMES, None), P(NAMES))
    return jax.shard_map(
        functools.partial(body, sizes), mesh=fine, in_specs=in_specs, out_specs=out_specs, check_vma=False
    )
```

```python
import functools
import jax
import jax.numpy as jnp
import numpy as np
from jax import lax
from jax.experimental import pallas as pl
from jax.experimental.pallas import tpu as pltpu
from jax.sharding import Mesh, PartitionSpec as P

SIZES = (4, 4, 4, 2, 3, 2)
NAMES = ("zh", "x", "yh", "yl", "zl", "c")
PAD = 128


VMEM = pl.BlockSpec(memory_space=pltpu.VMEM)


def parameters(mib):
    return pltpu.CompilerParams(vmem_limit_bytes=mib * 1024 * 1024)


def quotient(values, divisor, bound):
    shift = 16
    factor = -(-(1 << shift) // divisor)
    assert all(v * factor >> shift == v // divisor for v in range(bound))
    return (values * factor) >> shift


def source_rows(sizes, core):
    _, x, yh, yl, zl, _ = sizes
    stride = {"s": 1, "zl": 4, "yl": 4 * zl, "yh": 4 * zl * yl, "x": 4 * zl * yl * yh, "zh": 4 * zl * yl * yh * x}
    bound = 8 * x * yh * yl * zl
    left = lax.broadcasted_iota(jnp.int32, (bound, 1), 0)
    source = jnp.zeros((bound, 1), jnp.int32)
    for name, size in (("yh", yh), ("zh", 2), ("zl", zl), ("yl", yl), ("x", x), ("s", 2)):
        over = quotient(left, size, bound)
        source = source + (left - over * size) * stride[name]
        left, bound = over, bound // size
    return source + 2 * jnp.where(left == 0, 1 - core, core)


def split_pairs(values):
    lane = lax.broadcasted_iota(jnp.int32, (values[0].shape[0], PAD), 1)
    parts = jnp.zeros(lane.shape, jnp.float32)
    for s, value in enumerate(values):
        high = value.astype(jnp.bfloat16).astype(jnp.float32)
        parts = jnp.where(lane == 2 * s, high, parts)
        parts = jnp.where(lane == 2 * s + 1, value - high, parts)
    return parts


def join_pairs(parts):
    lane = lax.broadcasted_iota(jnp.int32, parts.shape, 1)
    return [
        jnp.sum(jnp.where((lane == 2 * s) | (lane == 2 * s + 1), parts, 0.0), axis=1, keepdims=True)
        for s in range(2)
    ]


def term_kernel(sizes, grad_ref, ctx_ref, send_ref, keep_ref, acc):
    span = grad_ref.shape[1] // 2
    width = ctx_ref.shape[1]
    blocks, part = send_ref.shape[0], send_ref.shape[1] // 2
    column = lax.broadcasted_iota(jnp.int32, (span, span), 1)
    pick = jnp.where(source_rows(sizes, lax.axis_index("c")) == column, 1.0, 0.0).astype(jnp.bfloat16)
    ones = jnp.ones((ctx_ref.shape[0], PAD), jnp.bfloat16)
    for step in range(2):
        moved = lax.dot_general(
            pick,
            grad_ref[:, step * span : (step + 1) * span],
            (((1,), (1,)), ((), ())),
            preferred_element_type=jnp.float32,
        ).astype(jnp.bfloat16)
        acc[step, :, :width] = jnp.dot(moved, ctx_ref[...], preferred_element_type=jnp.float32)
        acc[step, :, width:] = jnp.dot(moved, ones, preferred_element_type=jnp.float32)
    for side, out in enumerate((send_ref, keep_ref)):
        for block in range(blocks):
            sums = []
            for s in range(2):
                at = ((side * 2 + s) * blocks + block) * part
                both = jnp.concatenate([acc[0, at : at + part, :], acc[1, at : at + part, :]], axis=0)
                out[block, :, s * width : (s + 1) * width] = both[:, :width].astype(jnp.bfloat16)
                sums.append(both[:, width:])
            out[block, :, 2 * width :] = split_pairs(sums).astype(jnp.bfloat16)


def local_terms(sizes, grad_out, context):
    zh, x, yh, yl, zl, _ = sizes
    width = context.shape[1]
    piece = jax.ShapeDtypeStruct((x * yl * zl, zh * yh, 2 * width + PAD), jnp.bfloat16)
    return pl.pallas_call(
        functools.partial(term_kernel, sizes),
        out_shape=(piece, piece),
        in_specs=[VMEM] * 2,
        out_specs=(VMEM, VMEM),
        scratch_shapes=[pltpu.VMEM((2, grad_out.shape[1] // 2, width + PAD), jnp.float32)],
        compiler_params=parameters(40),
        cost_estimate=pl.CostEstimate(flops=4 * 10**9, bytes_accessed=5 * 10**6, transcendentals=0),
    )(grad_out, context)


def chip_kernel(got_ref, keep_ref, out_ref):
    wide = out_ref.shape[2] - PAD
    for block in range(out_ref.shape[0]):
        total = got_ref[block].astype(jnp.float32) + keep_ref[block].astype(jnp.float32)
        out_ref[block, :, :wide] = total[:, :wide].astype(out_ref.dtype)
        out_ref[block, :, wide:] = split_pairs(join_pairs(total[:, wide:])).astype(out_ref.dtype)


def chip_sum(got, keep):
    return pl.pallas_call(
        chip_kernel,
        out_shape=jax.ShapeDtypeStruct(got.shape, got.dtype),
        in_specs=[VMEM] * 2,
        out_specs=VMEM,
        compiler_params=parameters(16),
        cost_estimate=pl.CostEstimate(flops=10**6, bytes_accessed=4 * 10**6, transcendentals=0),
    )(got, keep)


def near_kernel(got_ref, *refs):
    sum_ref, wide = refs[-2:]
    for chunk in range(sum_ref.shape[1]):
        lanes = slice(chunk * PAD, (chunk + 1) * PAD)
        total = got_ref[0, :, lanes].astype(jnp.float32)
        for index in range(1, got_ref.shape[0]):
            total = total + got_ref[index, :, lanes].astype(jnp.float32)
        if chunk == sum_ref.shape[1] - 1:
            total = split_pairs(join_pairs(total))
        wide[:, chunk, :] = total
    sum_ref[...] = wide[...].astype(sum_ref.dtype)


def near_sum(got, held):
    _, rows, lanes = got.shape
    shape = (rows, lanes // PAD, PAD)
    return pl.pallas_call(
        near_kernel,
        out_shape=jax.ShapeDtypeStruct(shape, jnp.bfloat16),
        in_specs=[VMEM] + [pl.BlockSpec(memory_space=pl.ANY)] * len(held),
        out_specs=VMEM,
        scratch_shapes=[pltpu.VMEM(shape, jnp.float32)],
        compiler_params=parameters(16),
        cost_estimate=pl.CostEstimate(flops=10**6, bytes_accessed=2 * 10**6, transcendentals=0),
    )(got, *held)


def last_kernel(scale, far_ref, weight_ref, bias_ref):
    total = far_ref[0].astype(jnp.float32)
    for index in range(1, far_ref.shape[0]):
        total = total + far_ref[index].astype(jnp.float32)
    total = total * scale
    chunks = (total.shape[0] - 1) // 2
    for s in range(2):
        for chunk in range(chunks):
            at = s * chunks + chunk
            weight_ref[s : s + 1, chunk * PAD : (chunk + 1) * PAD] = total[at : at + 1, :]
    tail = total[2 * chunks : 2 * chunks + 1, :]
    lane = lax.broadcasted_iota(jnp.int32, (1, PAD), 1)
    for s in range(2):
        bias_ref[s] = jnp.sum(jnp.where((lane == 2 * s) | (lane == 2 * s + 1), tail, 0.0))


def last_sum(far, scale):
    width = (far.shape[1] - 1) // 2 * PAD
    return pl.pallas_call(
        functools.partial(last_kernel, scale),
        out_shape=(jax.ShapeDtypeStruct((2, width), jnp.float32), jax.ShapeDtypeStruct((2,), jnp.float32)),
        in_specs=[VMEM],
        out_specs=(pl.BlockSpec((2, width), lambda: (0, 0)), pl.BlockSpec(memory_space=pltpu.SMEM)),
        compiler_params=parameters(16),
        cost_estimate=pl.CostEstimate(flops=10**5, bytes_accessed=2 * 10**5, transcendentals=0),
    )(far)


def ctx_kernel(chips, grad_ref, *refs):
    held, out_ref = refs[:-1], refs[-1]
    chip, core = lax.axis_index("zl"), lax.axis_index("c")
    rows = held[0].shape[0]
    total = None
    for slot, block in enumerate(held):
        owner = lax.rem(chip + chips - slot % chips, chips)
        side = core if slot < chips else 1 - core
        at = pl.multiple_of((2 * owner + side) * rows, rows)
        product = jnp.dot(grad_ref[:, pl.ds(at, rows)], block[...], preferred_element_type=jnp.float32)
        total = product if total is None else total + product
    out_ref[...] = total.astype(out_ref.dtype)


def ctx_product(chips, grad_out, held):
    tokens, depth = grad_out.shape
    width = held[0].shape[1]
    steps = 2
    return pl.pallas_call(
        functools.partial(ctx_kernel, chips),
        out_shape=jax.ShapeDtypeStruct((tokens, width), jnp.bfloat16),
        grid=(steps,),
        in_specs=[pl.BlockSpec((tokens // steps, depth), lambda i: (i, 0))] + [VMEM] * len(held),
        out_specs=pl.BlockSpec((tokens // steps, width), lambda i: (i, 0)),
        compiler_params=parameters(24),
        cost_estimate=pl.CostEstimate(flops=12 * 10**8, bytes_accessed=5 * 10**6, transcendentals=0),
    )(grad_out, *held)


def body(sizes, grad_out, context, codes, scales):
    count = int(np.prod(sizes))
    chips = sizes[4]
    ring = sizes[0] * chips
    swap = [(0, 1), (1, 0)]

    send, keep = local_terms(sizes, grad_out, context)
    got = lax.ppermute(send, "c", swap)
    block = (codes[0].astype(jnp.float32) * scales.astype(jnp.float32)).astype(jnp.bfloat16)
    held = [block]
    for back in range(1, chips):
        hop = back if back <= chips // 2 else back - chips
        held.append(lax.ppermute(block, ("zh", "zl"), [(i, (i + hop) % ring) for i in range(ring)]))
    held += [lax.ppermute(piece, "c", swap) for piece in held]

    near = lax.all_to_all(chip_sum(got, keep), ("x", "yl", "zl"), split_axis=0, concat_axis=0, tiled=True)
    near = near_sum(near, held[1:])
    far = lax.all_to_all(near, ("zh", "yh"), split_axis=0, concat_axis=0, tiled=True)
    weight_grad, bias_grad = last_sum(far, 1.0 / count)

    ctx_grad = ctx_product(chips, grad_out, held)
    return ctx_grad, weight_grad, bias_grad


def solution(mesh, sizes=SIZES):
    fine = Mesh(mesh.devices.reshape(sizes), NAMES)
    in_specs = (P(NAMES, None), P(NAMES, None), P(("zl", "c"), None, None), P(("zl", "c"), None))
    out_specs = (P(NAMES, None), P(NAMES, None), P(NAMES))
    return jax.shard_map(
        functools.partial(body, sizes), mesh=fine, in_specs=in_specs, out_specs=out_specs, check_vma=False
    )
```

```python
import functools
import jax
import jax.numpy as jnp
import numpy as np
from jax import lax
from jax.experimental import pallas as pl
from jax.experimental.pallas import tpu as pltpu
from jax.sharding import Mesh, PartitionSpec as P

SIZES = (4, 4, 4, 2, 3, 2)
NAMES = ("zh", "x", "yh", "yl", "zl", "c")
PAD = 128


VMEM = pl.BlockSpec(memory_space=pltpu.VMEM)


def parameters(mib):
    return pltpu.CompilerParams(vmem_limit_bytes=mib * 1024 * 1024)


def quotient(values, divisor, bound):
    shift = 16
    factor = -(-(1 << shift) // divisor)
    assert all(v * factor >> shift == v // divisor for v in range(bound))
    return (values * factor) >> shift


def source_rows(sizes, core):
    _, x, yh, yl, zl, _ = sizes
    stride = {"s": 1, "zl": 4, "yl": 4 * zl, "yh": 4 * zl * yl, "x": 4 * zl * yl * yh, "zh": 4 * zl * yl * yh * x}
    bound = 8 * x * yh * yl * zl
    left = lax.broadcasted_iota(jnp.int32, (bound, 1), 0)
    source = jnp.zeros((bound, 1), jnp.int32)
    for name, size in (("zl", zl), ("yh", yh), ("zh", 2), ("yl", yl), ("x", x), ("s", 2)):
        over = quotient(left, size, bound)
        source = source + (left - over * size) * stride[name]
        left, bound = over, bound // size
    return source + 2 * jnp.where(left == 0, 1 - core, core)


def split_pairs(values):
    lane = lax.broadcasted_iota(jnp.int32, (values[0].shape[0], PAD), 1)
    parts = jnp.zeros(lane.shape, jnp.float32)
    for s, value in enumerate(values):
        high = value.astype(jnp.bfloat16).astype(jnp.float32)
        parts = jnp.where(lane == 2 * s, high, parts)
        parts = jnp.where(lane == 2 * s + 1, value - high, parts)
    return parts


def join_pairs(parts):
    lane = lax.broadcasted_iota(jnp.int32, parts.shape, 1)
    return [
        jnp.sum(jnp.where((lane == 2 * s) | (lane == 2 * s + 1), parts, 0.0), axis=1, keepdims=True)
        for s in range(2)
    ]


def term_kernel(sizes, grad_ref, ctx_ref, send_ref, keep_ref, acc):
    span = grad_ref.shape[1] // 2
    width = ctx_ref.shape[1]
    blocks, part = send_ref.shape[0], send_ref.shape[1] // 2
    column = lax.broadcasted_iota(jnp.int32, (span, span), 1)
    pick = jnp.where(source_rows(sizes, lax.axis_index("c")) == column, 1.0, 0.0).astype(jnp.bfloat16)
    ones = jnp.ones((ctx_ref.shape[0], PAD), jnp.bfloat16)
    for step in range(2):
        moved = lax.dot_general(
            pick,
            grad_ref[:, step * span : (step + 1) * span],
            (((1,), (1,)), ((), ())),
            preferred_element_type=jnp.float32,
        ).astype(jnp.bfloat16)
        acc[step, :, :width] = jnp.dot(moved, ctx_ref[...], preferred_element_type=jnp.float32)
        acc[step, :, width:] = jnp.dot(moved, ones, preferred_element_type=jnp.float32)
    for side, out in enumerate((send_ref, keep_ref)):
        for block in range(blocks):
            sums = []
            for s in range(2):
                at = ((side * 2 + s) * blocks + block) * part
                both = jnp.concatenate([acc[0, at : at + part, :], acc[1, at : at + part, :]], axis=0)
                out[block, :, s * width : (s + 1) * width] = both[:, :width].astype(jnp.bfloat16)
                sums.append(both[:, width:])
            out[block, :, 2 * width :] = split_pairs(sums).astype(jnp.bfloat16)


def local_terms(sizes, grad_out, context):
    zh, x, yh, yl, zl, _ = sizes
    width = context.shape[1]
    piece = jax.ShapeDtypeStruct((x * yl, zh * yh * zl, 2 * width + PAD), jnp.bfloat16)
    return pl.pallas_call(
        functools.partial(term_kernel, sizes),
        out_shape=(piece, piece),
        in_specs=[VMEM] * 2,
        out_specs=(VMEM, VMEM),
        scratch_shapes=[pltpu.VMEM((2, grad_out.shape[1] // 2, width + PAD), jnp.float32)],
        compiler_params=parameters(40),
        cost_estimate=pl.CostEstimate(flops=4 * 10**9, bytes_accessed=5 * 10**6, transcendentals=0),
    )(grad_out, context)


def chip_kernel(got_ref, keep_ref, out_ref):
    wide = out_ref.shape[2] - PAD
    for block in range(out_ref.shape[0]):
        total = got_ref[block].astype(jnp.float32) + keep_ref[block].astype(jnp.float32)
        out_ref[block, :, :wide] = total[:, :wide].astype(out_ref.dtype)
        out_ref[block, :, wide:] = split_pairs(join_pairs(total[:, wide:])).astype(out_ref.dtype)


def chip_sum(got, keep):
    return pl.pallas_call(
        chip_kernel,
        out_shape=jax.ShapeDtypeStruct(got.shape, got.dtype),
        in_specs=[VMEM] * 2,
        out_specs=VMEM,
        compiler_params=parameters(16),
        cost_estimate=pl.CostEstimate(flops=10**6, bytes_accessed=4 * 10**6, transcendentals=0),
    )(got, keep)


def near_kernel(got_ref, *refs):
    sum_ref, wide = refs[-2:]
    for chunk in range(sum_ref.shape[1]):
        lanes = slice(chunk * PAD, (chunk + 1) * PAD)
        total = got_ref[0, :, lanes].astype(jnp.float32)
        for index in range(1, got_ref.shape[0]):
            total = total + got_ref[index, :, lanes].astype(jnp.float32)
        if chunk == sum_ref.shape[1] - 1:
            total = split_pairs(join_pairs(total))
        wide[:, chunk, :] = total
    sum_ref[...] = wide[...].astype(sum_ref.dtype)


def near_sum(got, held):
    _, rows, lanes = got.shape
    shape = (rows, lanes // PAD, PAD)
    return pl.pallas_call(
        near_kernel,
        out_shape=jax.ShapeDtypeStruct(shape, jnp.bfloat16),
        in_specs=[VMEM] + [pl.BlockSpec(memory_space=pl.ANY)] * len(held),
        out_specs=VMEM,
        scratch_shapes=[pltpu.VMEM(shape, jnp.float32)],
        compiler_params=parameters(16),
        cost_estimate=pl.CostEstimate(flops=10**6, bytes_accessed=2 * 10**6, transcendentals=0),
    )(got, *held)


def last_kernel(scale, far_ref, weight_ref, bias_ref):
    total = far_ref[0].astype(jnp.float32)
    for index in range(1, far_ref.shape[0]):
        total = total + far_ref[index].astype(jnp.float32)
    total = total * scale
    chunks = (total.shape[0] - 1) // 2
    for s in range(2):
        for chunk in range(chunks):
            at = s * chunks + chunk
            weight_ref[s : s + 1, chunk * PAD : (chunk + 1) * PAD] = total[at : at + 1, :]
    tail = total[2 * chunks : 2 * chunks + 1, :]
    lane = lax.broadcasted_iota(jnp.int32, (1, PAD), 1)
    for s in range(2):
        bias_ref[s] = jnp.sum(jnp.where((lane == 2 * s) | (lane == 2 * s + 1), tail, 0.0))


def last_sum(far, scale):
    width = (far.shape[1] - 1) // 2 * PAD
    return pl.pallas_call(
        functools.partial(last_kernel, scale),
        out_shape=(jax.ShapeDtypeStruct((2, width), jnp.float32), jax.ShapeDtypeStruct((2,), jnp.float32)),
        in_specs=[VMEM],
        out_specs=(pl.BlockSpec((2, width), lambda: (0, 0)), pl.BlockSpec(memory_space=pltpu.SMEM)),
        compiler_params=parameters(16),
        cost_estimate=pl.CostEstimate(flops=10**5, bytes_accessed=2 * 10**5, transcendentals=0),
    )(far)


def ctx_kernel(chips, grad_ref, *refs):
    held, out_ref = refs[:-1], refs[-1]
    chip, core = lax.axis_index("zl"), lax.axis_index("c")
    rows = held[0].shape[0]
    total = None
    for slot, block in enumerate(held):
        owner = lax.rem(chip + chips - slot % chips, chips)
        side = core if slot < chips else 1 - core
        at = pl.multiple_of((2 * owner + side) * rows, rows)
        product = jnp.dot(grad_ref[:, pl.ds(at, rows)], block[...], preferred_element_type=jnp.float32)
        total = product if total is None else total + product
    out_ref[...] = total.astype(out_ref.dtype)


def ctx_product(chips, grad_out, held):
    tokens, depth = grad_out.shape
    width = held[0].shape[1]
    steps = 2
    return pl.pallas_call(
        functools.partial(ctx_kernel, chips),
        out_shape=jax.ShapeDtypeStruct((tokens, width), jnp.bfloat16),
        grid=(steps,),
        in_specs=[pl.BlockSpec((tokens // steps, depth), lambda i: (i, 0))] + [VMEM] * len(held),
        out_specs=pl.BlockSpec((tokens // steps, width), lambda i: (i, 0)),
        compiler_params=parameters(24),
        cost_estimate=pl.CostEstimate(flops=12 * 10**8, bytes_accessed=5 * 10**6, transcendentals=0),
    )(grad_out, *held)


def body(sizes, grad_out, context, codes, scales):
    count = int(np.prod(sizes))
    chips = sizes[4]
    ring = sizes[0] * chips
    swap = [(0, 1), (1, 0)]

    send, keep = local_terms(sizes, grad_out, context)
    got = lax.ppermute(send, "c", swap)
    block = (codes[0].astype(jnp.float32) * scales.astype(jnp.float32)).astype(jnp.bfloat16)
    held = [block]
    for back in range(1, chips):
        hop = back if back <= chips // 2 else back - chips
        held.append(lax.ppermute(block, ("zh", "zl"), [(i, (i + hop) % ring) for i in range(ring)]))
    held += [lax.ppermute(piece, "c", swap) for piece in held]

    near = lax.all_to_all(chip_sum(got, keep), ("x", "yl"), split_axis=0, concat_axis=0, tiled=True)
    near = near_sum(near, held[1:])
    far = lax.all_to_all(near, ("zh", "yh", "zl"), split_axis=0, concat_axis=0, tiled=True)
    weight_grad, bias_grad = last_sum(far, 1.0 / count)

    ctx_grad = ctx_product(chips, grad_out, held)
    return ctx_grad, weight_grad, bias_grad


def solution(mesh, sizes=SIZES):
    fine = Mesh(mesh.devices.reshape(sizes), NAMES)
    in_specs = (P(NAMES, None), P(NAMES, None), P(("zl", "c"), None, None), P(("zl", "c"), None))
    out_specs = (P(NAMES, None), P(NAMES, None), P(NAMES))
    return jax.shard_map(
        functools.partial(body, sizes), mesh=fine, in_specs=in_specs, out_specs=out_specs, check_vma=False
    )
```

```python
import functools
import jax
import jax.numpy as jnp
import numpy as np
from jax import lax
from jax.experimental import pallas as pl
from jax.experimental.pallas import tpu as pltpu
from jax.sharding import Mesh, PartitionSpec as P

SIZES = (4, 4, 4, 2, 3, 2)
NAMES = ("zh", "x", "yh", "yl", "zl", "c")
PAD = 128


VMEM = pl.BlockSpec(memory_space=pltpu.VMEM)


def parameters(mib):
    return pltpu.CompilerParams(vmem_limit_bytes=mib * 1024 * 1024)


def quotient(values, divisor, bound):
    shift = 16
    factor = -(-(1 << shift) // divisor)
    assert all(v * factor >> shift == v // divisor for v in range(bound))
    return (values * factor) >> shift


def source_rows(sizes, core):
    _, x, yh, yl, zl, _ = sizes
    stride = {"s": 1, "zl": 4, "yl": 4 * zl, "yh": 4 * zl * yl, "x": 4 * zl * yl * yh, "zh": 4 * zl * yl * yh * x}
    bound = 8 * x * yh * yl * zl
    left = lax.broadcasted_iota(jnp.int32, (bound, 1), 0)
    source = jnp.zeros((bound, 1), jnp.int32)
    for name, size in (("zl", zl), ("yh", yh), ("zh", 2), ("yl", yl), ("x", x), ("s", 2)):
        over = quotient(left, size, bound)
        source = source + (left - over * size) * stride[name]
        left, bound = over, bound // size
    return source + 2 * jnp.where(left == 0, 1 - core, core)


def split_pairs(values):
    lane = lax.broadcasted_iota(jnp.int32, (values[0].shape[0], PAD), 1)
    parts = jnp.zeros(lane.shape, jnp.float32)
    for s, value in enumerate(values):
        high = value.astype(jnp.bfloat16).astype(jnp.float32)
        parts = jnp.where(lane == 2 * s, high, parts)
        parts = jnp.where(lane == 2 * s + 1, value - high, parts)
    return parts


def join_pairs(parts):
    lane = lax.broadcasted_iota(jnp.int32, parts.shape, 1)
    return [
        jnp.sum(jnp.where((lane == 2 * s) | (lane == 2 * s + 1), parts, 0.0), axis=1, keepdims=True)
        for s in range(2)
    ]


def term_kernel(sizes, grad_ref, ctx_ref, send_ref, keep_ref, acc):
    span = grad_ref.shape[1] // 2
    width = ctx_ref.shape[1]
    blocks, part = send_ref.shape[0], send_ref.shape[1] // 2
    column = lax.broadcasted_iota(jnp.int32, (span, span), 1)
    pick = jnp.where(source_rows(sizes, lax.axis_index("c")) == column, 1.0, 0.0).astype(jnp.bfloat16)
    ones = jnp.ones((ctx_ref.shape[0], PAD), jnp.bfloat16)
    for step in range(2):
        moved = lax.dot_general(
            pick,
            grad_ref[:, step * span : (step + 1) * span],
            (((1,), (1,)), ((), ())),
            preferred_element_type=jnp.float32,
        ).astype(jnp.bfloat16)
        acc[step, :, :width] = jnp.dot(moved, ctx_ref[...], preferred_element_type=jnp.float32)
        acc[step, :, width:] = jnp.dot(moved, ones, preferred_element_type=jnp.float32)
    for side, out in enumerate((send_ref, keep_ref)):
        for block in range(blocks):
            sums = []
            for s in range(2):
                at = ((side * 2 + s) * blocks + block) * part
                both = jnp.concatenate([acc[0, at : at + part, :], acc[1, at : at + part, :]], axis=0)
                out[block, :, s * width : (s + 1) * width] = both[:, :width].astype(jnp.bfloat16)
                sums.append(both[:, width:])
            out[block, :, 2 * width :] = split_pairs(sums).astype(jnp.bfloat16)


def local_terms(sizes, grad_out, context):
    zh, x, yh, yl, zl, _ = sizes
    width = context.shape[1]
    piece = jax.ShapeDtypeStruct((x * yl, zh * yh * zl, 2 * width + PAD), jnp.bfloat16)
    return pl.pallas_call(
        functools.partial(term_kernel, sizes),
        out_shape=(piece, piece),
        in_specs=[VMEM] * 2,
        out_specs=(VMEM, VMEM),
        scratch_shapes=[pltpu.VMEM((2, grad_out.shape[1] // 2, width + PAD), jnp.float32)],
        compiler_params=parameters(40),
        cost_estimate=pl.CostEstimate(flops=4 * 10**9, bytes_accessed=5 * 10**6, transcendentals=0),
    )(grad_out, context)


def chip_kernel(got_ref, keep_ref, out_ref):
    wide = out_ref.shape[2] - PAD
    for block in range(out_ref.shape[0]):
        total = got_ref[block].astype(jnp.float32) + keep_ref[block].astype(jnp.float32)
        out_ref[block, :, :wide] = total[:, :wide].astype(out_ref.dtype)
        out_ref[block, :, wide:] = split_pairs(join_pairs(total[:, wide:])).astype(out_ref.dtype)


def chip_sum(got, keep):
    return pl.pallas_call(
        chip_kernel,
        out_shape=jax.ShapeDtypeStruct(got.shape, got.dtype),
        in_specs=[VMEM] * 2,
        out_specs=VMEM,
        compiler_params=parameters(16),
        cost_estimate=pl.CostEstimate(flops=10**6, bytes_accessed=4 * 10**6, transcendentals=0),
    )(got, keep)


def near_kernel(got_ref, sum_ref, wide):
    for chunk in range(sum_ref.shape[1]):
        lanes = slice(chunk * PAD, (chunk + 1) * PAD)
        total = got_ref[0, :, lanes].astype(jnp.float32)
        for index in range(1, got_ref.shape[0]):
            total = total + got_ref[index, :, lanes].astype(jnp.float32)
        if chunk == sum_ref.shape[1] - 1:
            total = split_pairs(join_pairs(total))
        wide[:, chunk, :] = total
    sum_ref[...] = wide[...].astype(sum_ref.dtype)


def near_sum(got):
    _, rows, lanes = got.shape
    shape = (rows, lanes // PAD, PAD)
    return pl.pallas_call(
        near_kernel,
        out_shape=jax.ShapeDtypeStruct(shape, jnp.bfloat16),
        in_specs=[VMEM],
        out_specs=VMEM,
        scratch_shapes=[pltpu.VMEM(shape, jnp.float32)],
        compiler_params=parameters(16),
        cost_estimate=pl.CostEstimate(flops=10**6, bytes_accessed=2 * 10**6, transcendentals=0),
    )(got)


def last_kernel(scale, far_ref, weight_ref, bias_ref):
    total = far_ref[0].astype(jnp.float32)
    for index in range(1, far_ref.shape[0]):
        total = total + far_ref[index].astype(jnp.float32)
    total = total * scale
    chunks = (total.shape[0] - 1) // 2
    for s in range(2):
        for chunk in range(chunks):
            at = s * chunks + chunk
            weight_ref[s : s + 1, chunk * PAD : (chunk + 1) * PAD] = total[at : at + 1, :]
    tail = total[2 * chunks : 2 * chunks + 1, :]
    lane = lax.broadcasted_iota(jnp.int32, (1, PAD), 1)
    for s in range(2):
        bias_ref[s] = jnp.sum(jnp.where((lane == 2 * s) | (lane == 2 * s + 1), tail, 0.0))


def last_sum(far, scale):
    width = (far.shape[1] - 1) // 2 * PAD
    return pl.pallas_call(
        functools.partial(last_kernel, scale),
        out_shape=(jax.ShapeDtypeStruct((2, width), jnp.float32), jax.ShapeDtypeStruct((2,), jnp.float32)),
        in_specs=[VMEM],
        out_specs=(pl.BlockSpec((2, width), lambda: (0, 0)), pl.BlockSpec(memory_space=pltpu.SMEM)),
        compiler_params=parameters(16),
        cost_estimate=pl.CostEstimate(flops=10**5, bytes_accessed=2 * 10**5, transcendentals=0),
    )(far)


def ctx_kernel(chips, grad_ref, *refs):
    held, out_ref = refs[:-1], refs[-1]
    chip, core = lax.axis_index("zl"), lax.axis_index("c")
    rows = held[0].shape[0]
    total = None
    for slot, block in enumerate(held):
        owner = lax.rem(chip + chips - slot % chips, chips)
        side = core if slot < chips else 1 - core
        at = pl.multiple_of((2 * owner + side) * rows, rows)
        product = jnp.dot(grad_ref[:, pl.ds(at, rows)], block[...], preferred_element_type=jnp.float32)
        total = product if total is None else total + product
    out_ref[...] = total.astype(out_ref.dtype)


def ctx_product(chips, grad_out, held):
    tokens, depth = grad_out.shape
    width = held[0].shape[1]
    steps = 2
    return pl.pallas_call(
        functools.partial(ctx_kernel, chips),
        out_shape=jax.ShapeDtypeStruct((tokens, width), jnp.bfloat16),
        grid=(steps,),
        in_specs=[pl.BlockSpec((tokens // steps, depth), lambda i: (i, 0))] + [VMEM] * len(held),
        out_specs=pl.BlockSpec((tokens // steps, width), lambda i: (i, 0)),
        compiler_params=parameters(24),
        cost_estimate=pl.CostEstimate(flops=12 * 10**8, bytes_accessed=5 * 10**6, transcendentals=0),
    )(grad_out, *held)


def body(sizes, grad_out, context, codes, scales):
    count = int(np.prod(sizes))
    chips = sizes[4]
    ring = sizes[0] * chips
    swap = [(0, 1), (1, 0)]

    send, keep = local_terms(sizes, grad_out, context)
    got = lax.ppermute(send, "c", swap)
    block = (codes[0].astype(jnp.float32) * scales.astype(jnp.float32)).astype(jnp.bfloat16)
    held = [block]
    for back in range(1, chips):
        hop = back if back <= chips // 2 else back - chips
        held.append(lax.ppermute(block, ("zh", "zl"), [(i, (i + hop) % ring) for i in range(ring)]))
    held += [lax.ppermute(piece, "c", swap) for piece in held]

    near = lax.all_to_all(chip_sum(got, keep), ("x", "yl"), split_axis=0, concat_axis=0, tiled=True)
    near = near_sum(near)
    far = lax.all_to_all(near, ("zh", "yh", "zl"), split_axis=0, concat_axis=0, tiled=True)
    weight_grad, bias_grad = last_sum(far, 1.0 / count)

    ctx_grad = ctx_product(chips, grad_out, held)
    return ctx_grad, weight_grad, bias_grad


def solution(mesh, sizes=SIZES):
    fine = Mesh(mesh.devices.reshape(sizes), NAMES)
    in_specs = (P(NAMES, None), P(NAMES, None), P(("zl", "c"), None, None), P(("zl", "c"), None))
    out_specs = (P(NAMES, None), P(NAMES, None), P(NAMES))
    return jax.shard_map(
        functools.partial(body, sizes), mesh=fine, in_specs=in_specs, out_specs=out_specs, check_vma=False
    )
```

```python
import functools
import jax
import jax.numpy as jnp
import numpy as np
from jax import lax
from jax.experimental import pallas as pl
from jax.experimental.pallas import tpu as pltpu
from jax.sharding import Mesh, PartitionSpec as P

SIZES = (4, 4, 4, 2, 3, 2)
NAMES = ("zh", "x", "yh", "yl", "zl", "c")
PAD = 128


VMEM = pl.BlockSpec(memory_space=pltpu.VMEM)


def parameters(mib):
    return pltpu.CompilerParams(vmem_limit_bytes=mib * 1024 * 1024)


def quotient(values, divisor, bound):
    shift = 16
    factor = -(-(1 << shift) // divisor)
    assert all(v * factor >> shift == v // divisor for v in range(bound))
    return (values * factor) >> shift


def source_rows(sizes, core):
    _, x, yh, yl, zl, _ = sizes
    stride = {"s": 1, "zl": 4, "yl": 4 * zl, "yh": 4 * zl * yl, "x": 4 * zl * yl * yh, "zh": 4 * zl * yl * yh * x}
    bound = 8 * x * yh * yl * zl
    left = lax.broadcasted_iota(jnp.int32, (bound, 1), 0)
    source = jnp.zeros((bound, 1), jnp.int32)
    for name, size in (("zl", zl), ("yh", yh), ("zh", 2), ("yl", yl), ("x", x), ("s", 2)):
        over = quotient(left, size, bound)
        source = source + (left - over * size) * stride[name]
        left, bound = over, bound // size
    return source + 2 * jnp.where(left == 0, 1 - core, core)


def split_pairs(values):
    lane = lax.broadcasted_iota(jnp.int32, (values[0].shape[0], PAD), 1)
    parts = jnp.zeros(lane.shape, jnp.float32)
    for s, value in enumerate(values):
        high = value.astype(jnp.bfloat16).astype(jnp.float32)
        parts = jnp.where(lane == 2 * s, high, parts)
        parts = jnp.where(lane == 2 * s + 1, value - high, parts)
    return parts


def join_pairs(parts):
    lane = lax.broadcasted_iota(jnp.int32, parts.shape, 1)
    return [
        jnp.sum(jnp.where((lane == 2 * s) | (lane == 2 * s + 1), parts, 0.0), axis=1, keepdims=True)
        for s in range(2)
    ]


def term_kernel(sizes, grad_ref, ctx_ref, send_ref, keep_ref, acc):
    span = grad_ref.shape[1] // 2
    width = ctx_ref.shape[1]
    blocks, part = send_ref.shape[0], send_ref.shape[1] // 2
    column = lax.broadcasted_iota(jnp.int32, (span, span), 1)
    pick = jnp.where(source_rows(sizes, lax.axis_index("c")) == column, 1.0, 0.0).astype(jnp.bfloat16)
    ones = jnp.ones((ctx_ref.shape[0], PAD), jnp.bfloat16)
    for step in range(2):
        moved = lax.dot_general(
            pick,
            grad_ref[:, step * span : (step + 1) * span],
            (((1,), (1,)), ((), ())),
            preferred_element_type=jnp.float32,
        ).astype(jnp.bfloat16)
        acc[step, :, :width] = jnp.dot(moved, ctx_ref[...], preferred_element_type=jnp.float32)
        acc[step, :, width:] = jnp.dot(moved, ones, preferred_element_type=jnp.float32)
    for side, out in enumerate((send_ref, keep_ref)):
        for block in range(blocks):
            sums = []
            for s in range(2):
                at = ((side * 2 + s) * blocks + block) * part
                both = jnp.concatenate([acc[0, at : at + part, :], acc[1, at : at + part, :]], axis=0)
                out[block, :, s * width : (s + 1) * width] = both[:, :width].astype(jnp.bfloat16)
                sums.append(both[:, width:])
            out[block, :, 2 * width :] = split_pairs(sums).astype(jnp.bfloat16)


def local_terms(sizes, grad_out, context):
    zh, x, yh, yl, zl, _ = sizes
    width = context.shape[1]
    piece = jax.ShapeDtypeStruct((x * yl, zh * yh * zl, 2 * width + PAD), jnp.bfloat16)
    return pl.pallas_call(
        functools.partial(term_kernel, sizes),
        out_shape=(piece, piece),
        in_specs=[VMEM] * 2,
        out_specs=(VMEM, VMEM),
        scratch_shapes=[pltpu.VMEM((2, grad_out.shape[1] // 2, width + PAD), jnp.float32)],
        compiler_params=parameters(40),
        cost_estimate=pl.CostEstimate(flops=4 * 10**9, bytes_accessed=5 * 10**6, transcendentals=0),
    )(grad_out, context)


def chip_kernel(got_ref, keep_ref, out_ref):
    wide = out_ref.shape[2] - PAD
    for block in range(out_ref.shape[0]):
        total = got_ref[block].astype(jnp.float32) + keep_ref[block].astype(jnp.float32)
        out_ref[block, :, :wide] = total[:, :wide].astype(out_ref.dtype)
        out_ref[block, :, wide:] = split_pairs(join_pairs(total[:, wide:])).astype(out_ref.dtype)


def chip_sum(got, keep):
    return pl.pallas_call(
        chip_kernel,
        out_shape=jax.ShapeDtypeStruct(got.shape, got.dtype),
        in_specs=[VMEM] * 2,
        out_specs=VMEM,
        compiler_params=parameters(16),
        cost_estimate=pl.CostEstimate(flops=10**6, bytes_accessed=4 * 10**6, transcendentals=0),
    )(got, keep)


def near_kernel(got_ref, sum_ref, wide):
    for chunk in range(sum_ref.shape[1]):
        lanes = slice(chunk * PAD, (chunk + 1) * PAD)
        total = got_ref[0, :, lanes].astype(jnp.float32)
        for index in range(1, got_ref.shape[0]):
            total = total + got_ref[index, :, lanes].astype(jnp.float32)
        if chunk == sum_ref.shape[1] - 1:
            total = split_pairs(join_pairs(total))
        wide[:, chunk, :] = total
    sum_ref[...] = wide[...].astype(sum_ref.dtype)


def near_sum(got):
    _, rows, lanes = got.shape
    shape = (rows, lanes // PAD, PAD)
    return pl.pallas_call(
        near_kernel,
        out_shape=jax.ShapeDtypeStruct(shape, jnp.bfloat16),
        in_specs=[VMEM],
        out_specs=VMEM,
        scratch_shapes=[pltpu.VMEM(shape, jnp.float32)],
        compiler_params=parameters(16),
        cost_estimate=pl.CostEstimate(flops=10**6, bytes_accessed=2 * 10**6, transcendentals=0),
    )(got)


def last_kernel(scale, far_ref, weight_ref, bias_ref):
    total = far_ref[0].astype(jnp.float32)
    for index in range(1, far_ref.shape[0]):
        total = total + far_ref[index].astype(jnp.float32)
    total = total * scale
    chunks = (total.shape[0] - 1) // 2
    for s in range(2):
        for chunk in range(chunks):
            at = s * chunks + chunk
            weight_ref[s : s + 1, chunk * PAD : (chunk + 1) * PAD] = total[at : at + 1, :]
    tail = total[2 * chunks : 2 * chunks + 1, :]
    lane = lax.broadcasted_iota(jnp.int32, (1, PAD), 1)
    for s in range(2):
        bias_ref[s] = jnp.sum(jnp.where((lane == 2 * s) | (lane == 2 * s + 1), tail, 0.0))


def last_sum(far, scale):
    width = (far.shape[1] - 1) // 2 * PAD
    return pl.pallas_call(
        functools.partial(last_kernel, scale),
        out_shape=(jax.ShapeDtypeStruct((2, width), jnp.float32), jax.ShapeDtypeStruct((2,), jnp.float32)),
        in_specs=[VMEM],
        out_specs=(pl.BlockSpec((2, width), lambda: (0, 0)), pl.BlockSpec(memory_space=pltpu.SMEM)),
        compiler_params=parameters(16),
        cost_estimate=pl.CostEstimate(flops=10**5, bytes_accessed=2 * 10**5, transcendentals=0),
    )(far)


def ctx_kernel(chips, grad_ref, *refs):
    held, out_ref = refs[:-1], refs[-1]
    chip, core = lax.axis_index("zl"), lax.axis_index("c")
    rows = held[0].shape[0]
    total = None
    for slot, block in enumerate(held):
        owner = lax.rem(chip + chips - slot % chips, chips)
        side = core if slot < chips else 1 - core
        at = pl.multiple_of((2 * owner + side) * rows, rows)
        product = jnp.dot(grad_ref[:, pl.ds(at, rows)], block[...], preferred_element_type=jnp.float32)
        total = product if total is None else total + product
    out_ref[...] = total.astype(out_ref.dtype)


def ctx_product(chips, grad_out, held):
    tokens, depth = grad_out.shape
    width = held[0].shape[1]
    steps = 2
    return pl.pallas_call(
        functools.partial(ctx_kernel, chips),
        out_shape=jax.ShapeDtypeStruct((tokens, width), jnp.bfloat16),
        grid=(steps,),
        in_specs=[pl.BlockSpec((tokens // steps, depth), lambda i: (i, 0))] + [VMEM] * len(held),
        out_specs=pl.BlockSpec((tokens // steps, width), lambda i: (i, 0)),
        compiler_params=parameters(24),
        cost_estimate=pl.CostEstimate(flops=12 * 10**8, bytes_accessed=5 * 10**6, transcendentals=0),
    )(grad_out, *held)


def body(sizes, grad_out, context, codes, scales):
    count = int(np.prod(sizes))
    chips = sizes[4]
    ring = sizes[0] * chips
    swap = [(0, 1), (1, 0)]

    send, keep = local_terms(sizes, grad_out, context)
    got = lax.ppermute(send, "c", swap)
    block = (codes[0].astype(jnp.float32) * scales.astype(jnp.float32)).astype(jnp.bfloat16)
    held = []
    for side in range(2):
        for back in range(chips):
            hop = back if back <= chips // 2 else back - chips
            moves = [(2 * i + c, 2 * ((i + hop) % ring) + (c ^ side)) for i in range(ring) for c in range(2)]
            held.append(lax.ppermute(block, ("zh", "zl", "c"), moves) if side + back else block)

    near = lax.all_to_all(chip_sum(got, keep), ("x", "yl"), split_axis=0, concat_axis=0, tiled=True)
    near = near_sum(near)
    far = lax.all_to_all(near, ("zh", "yh", "zl"), split_axis=0, concat_axis=0, tiled=True)
    weight_grad, bias_grad = last_sum(far, 1.0 / count)

    ctx_grad = ctx_product(chips, grad_out, held)
    return ctx_grad, weight_grad, bias_grad


def solution(mesh, sizes=SIZES):
    fine = Mesh(mesh.devices.reshape(sizes), NAMES)
    in_specs = (P(NAMES, None), P(NAMES, None), P(("zl", "c"), None, None), P(("zl", "c"), None))
    out_specs = (P(NAMES, None), P(NAMES, None), P(NAMES))
    return jax.shard_map(
        functools.partial(body, sizes), mesh=fine, in_specs=in_specs, out_specs=out_specs, check_vma=False
    )
```

```python
import functools
import jax
import jax.numpy as jnp
import numpy as np
from jax import lax
from jax.experimental import pallas as pl
from jax.experimental.pallas import tpu as pltpu
from jax.sharding import Mesh, PartitionSpec as P

SIZES = (4, 4, 4, 2, 3, 2)
NAMES = ("zh", "x", "yh", "yl", "zl", "c")
PAD = 128


VMEM = pl.BlockSpec(memory_space=pltpu.VMEM)


def parameters(mib):
    return pltpu.CompilerParams(vmem_limit_bytes=mib * 1024 * 1024)


def quotient(values, divisor, bound):
    shift = 16
    factor = -(-(1 << shift) // divisor)
    assert all(v * factor >> shift == v // divisor for v in range(bound))
    return (values * factor) >> shift


def source_rows(sizes, core):
    _, x, yh, yl, zl, _ = sizes
    stride = {"s": 1, "zl": 4, "yl": 4 * zl, "yh": 4 * zl * yl, "x": 4 * zl * yl * yh, "zh": 4 * zl * yl * yh * x}
    bound = 8 * x * yh * yl * zl
    left = lax.broadcasted_iota(jnp.int32, (bound, 1), 0)
    source = jnp.zeros((bound, 1), jnp.int32)
    for name, size in (("zl", zl), ("yh", yh), ("zh", 2), ("yl", yl), ("x", x), ("s", 2)):
        over = quotient(left, size, bound)
        source = source + (left - over * size) * stride[name]
        left, bound = over, bound // size
    return source + 2 * jnp.where(left == 0, 1 - core, core)


def split_pairs(values):
    lane = lax.broadcasted_iota(jnp.int32, (values[0].shape[0], PAD), 1)
    parts = jnp.zeros(lane.shape, jnp.float32)
    for s, value in enumerate(values):
        high = value.astype(jnp.bfloat16).astype(jnp.float32)
        parts = jnp.where(lane == 2 * s, high, parts)
        parts = jnp.where(lane == 2 * s + 1, value - high, parts)
    return parts


def join_pairs(parts):
    lane = lax.broadcasted_iota(jnp.int32, parts.shape, 1)
    return [
        jnp.sum(jnp.where((lane == 2 * s) | (lane == 2 * s + 1), parts, 0.0), axis=1, keepdims=True)
        for s in range(2)
    ]


def term_kernel(sizes, grad_ref, ctx_ref, send_ref, keep_ref, acc):
    span = grad_ref.shape[1] // 2
    width = ctx_ref.shape[1]
    blocks, part = send_ref.shape[0], send_ref.shape[1] // 2
    column = lax.broadcasted_iota(jnp.int32, (span, span), 1)
    pick = jnp.where(source_rows(sizes, lax.axis_index("c")) == column, 1.0, 0.0).astype(jnp.bfloat16)
    ones = jnp.ones((ctx_ref.shape[0], PAD), jnp.bfloat16)
    for step in range(2):
        moved = lax.dot_general(
            pick,
            grad_ref[:, step * span : (step + 1) * span],
            (((1,), (1,)), ((), ())),
            preferred_element_type=jnp.float32,
        ).astype(jnp.bfloat16)
        acc[step, :, :width] = jnp.dot(moved, ctx_ref[...], preferred_element_type=jnp.float32)
        acc[step, :, width:] = jnp.dot(moved, ones, preferred_element_type=jnp.float32)
    for side, out in enumerate((send_ref, keep_ref)):
        for block in range(blocks):
            sums = []
            for s in range(2):
                at = ((side * 2 + s) * blocks + block) * part
                both = jnp.concatenate([acc[0, at : at + part, :], acc[1, at : at + part, :]], axis=0)
                out[block, :, s * width : (s + 1) * width] = both[:, :width].astype(jnp.bfloat16)
                sums.append(both[:, width:])
            out[block, :, 2 * width :] = split_pairs(sums).astype(jnp.bfloat16)


def local_terms(sizes, grad_out, context):
    zh, x, yh, yl, zl, _ = sizes
    width = context.shape[1]
    piece = jax.ShapeDtypeStruct((x * yl, zh * yh * zl, 2 * width + PAD), jnp.bfloat16)
    return pl.pallas_call(
        functools.partial(term_kernel, sizes),
        out_shape=(piece, piece),
        in_specs=[VMEM] * 2,
        out_specs=(VMEM, VMEM),
        scratch_shapes=[pltpu.VMEM((2, grad_out.shape[1] // 2, width + PAD), jnp.float32)],
        compiler_params=parameters(40),
        cost_estimate=pl.CostEstimate(flops=4 * 10**9, bytes_accessed=5 * 10**6, transcendentals=0),
    )(grad_out, context)


def chip_kernel(got_ref, keep_ref, out_ref):
    wide = out_ref.shape[2] - PAD
    for block in range(out_ref.shape[0]):
        total = got_ref[block].astype(jnp.float32) + keep_ref[block].astype(jnp.float32)
        out_ref[block, :, :wide] = total[:, :wide].astype(out_ref.dtype)
        out_ref[block, :, wide:] = split_pairs(join_pairs(total[:, wide:])).astype(out_ref.dtype)


def chip_sum(got, keep):
    return pl.pallas_call(
        chip_kernel,
        out_shape=jax.ShapeDtypeStruct(got.shape, got.dtype),
        in_specs=[VMEM] * 2,
        out_specs=VMEM,
        compiler_params=parameters(16),
        cost_estimate=pl.CostEstimate(flops=10**6, bytes_accessed=4 * 10**6, transcendentals=0),
    )(got, keep)


def near_kernel(got_ref, sum_ref, wide):
    for chunk in range(sum_ref.shape[1]):
        lanes = slice(chunk * PAD, (chunk + 1) * PAD)
        total = got_ref[0, :, lanes].astype(jnp.float32)
        for index in range(1, got_ref.shape[0]):
            total = total + got_ref[index, :, lanes].astype(jnp.float32)
        if chunk == sum_ref.shape[1] - 1:
            total = split_pairs(join_pairs(total))
        wide[:, chunk, :] = total
    sum_ref[...] = wide[...].astype(sum_ref.dtype)


def near_sum(got):
    _, rows, lanes = got.shape
    shape = (rows, lanes // PAD, PAD)
    return pl.pallas_call(
        near_kernel,
        out_shape=jax.ShapeDtypeStruct(shape, jnp.bfloat16),
        in_specs=[VMEM],
        out_specs=VMEM,
        scratch_shapes=[pltpu.VMEM(shape, jnp.float32)],
        compiler_params=parameters(16),
        cost_estimate=pl.CostEstimate(flops=10**6, bytes_accessed=2 * 10**6, transcendentals=0),
    )(got)


def last_kernel(scale, far_ref, weight_ref, bias_ref):
    total = far_ref[0].astype(jnp.float32)
    for index in range(1, far_ref.shape[0]):
        total = total + far_ref[index].astype(jnp.float32)
    total = total * scale
    chunks = (total.shape[0] - 1) // 2
    for s in range(2):
        for chunk in range(chunks):
            at = s * chunks + chunk
            weight_ref[s : s + 1, chunk * PAD : (chunk + 1) * PAD] = total[at : at + 1, :]
    tail = total[2 * chunks : 2 * chunks + 1, :]
    lane = lax.broadcasted_iota(jnp.int32, (1, PAD), 1)
    for s in range(2):
        bias_ref[s] = jnp.sum(jnp.where((lane == 2 * s) | (lane == 2 * s + 1), tail, 0.0))


def last_sum(far, scale):
    width = (far.shape[1] - 1) // 2 * PAD
    return pl.pallas_call(
        functools.partial(last_kernel, scale),
        out_shape=(jax.ShapeDtypeStruct((2, width), jnp.float32), jax.ShapeDtypeStruct((2,), jnp.float32)),
        in_specs=[VMEM],
        out_specs=(pl.BlockSpec((2, width), lambda: (0, 0)), pl.BlockSpec(memory_space=pltpu.SMEM)),
        compiler_params=parameters(16),
        cost_estimate=pl.CostEstimate(flops=10**5, bytes_accessed=2 * 10**5, transcendentals=0),
    )(far)


def ctx_kernel(chips, slots, grad_ref, *refs):
    held, (*before, out_ref) = refs[: len(slots)], refs[len(slots) :]
    chip, core = lax.axis_index("zl"), lax.axis_index("c")
    rows = held[0].shape[0]
    total = before[0][...] if before else None
    for (back, other), block in zip(slots, held):
        owner = lax.rem(chip + chips - back, chips)
        side = 1 - core if other else core
        at = pl.multiple_of((2 * owner + side) * rows, rows)
        product = jnp.dot(grad_ref[:, pl.ds(at, rows)], block[...], preferred_element_type=jnp.float32)
        total = product if total is None else total + product
    out_ref[...] = total.astype(out_ref.dtype)


def ctx_product(chips, kind, grad_out, held, *before):
    tokens, depth = grad_out.shape
    steps = 2

    def rows(width):
        return pl.BlockSpec((tokens // steps, width), lambda i: (i, 0))

    blocks = list(held.values())
    width = blocks[0].shape[1]
    return pl.pallas_call(
        functools.partial(ctx_kernel, chips, tuple(held)),
        out_shape=jax.ShapeDtypeStruct((tokens, width), kind),
        grid=(steps,),
        in_specs=[rows(depth)] + [VMEM] * len(blocks) + [rows(width)] * len(before),
        out_specs=rows(width),
        compiler_params=parameters(24),
        cost_estimate=pl.CostEstimate(flops=len(blocks) * 2 * 10**8, bytes_accessed=4 * 10**6, transcendentals=0),
    )(grad_out, *blocks, *before)


def body(sizes, grad_out, context, codes, scales):
    count = int(np.prod(sizes))
    chips = sizes[4]
    ring = sizes[0] * chips
    swap = [(0, 1), (1, 0)]

    send, keep = local_terms(sizes, grad_out, context)
    got = lax.ppermute(send, "c", swap)
    block = (codes[0].astype(jnp.float32) * scales.astype(jnp.float32)).astype(jnp.bfloat16)
    held = {(0, False): block, (0, True): lax.ppermute(block, "c", swap)}
    for back in range(1, chips):
        hop = back if back <= chips // 2 else back - chips
        moves = [(i, (i + hop) % ring) for i in range(ring)]
        held[back, False] = lax.ppermute(block, ("zh", "zl"), moves)

    near = lax.all_to_all(chip_sum(got, keep), ("x", "yl"), split_axis=0, concat_axis=0, tiled=True)
    near = near_sum(near)
    _, held = lax.optimization_barrier((near, held))
    far = lax.all_to_all(near, ("zh", "yh", "zl"), split_axis=0, concat_axis=0, tiled=True)
    weight_grad, bias_grad = last_sum(far, 1.0 / count)

    part = ctx_product(chips, jnp.float32, grad_out, held)
    part, held = lax.optimization_barrier((part, held))
    late = {(back, True): lax.ppermute(held[back, False], "c", swap) for back in range(1, chips)}
    ctx_grad = ctx_product(chips, jnp.bfloat16, grad_out, late, part)
    return ctx_grad, weight_grad, bias_grad


def solution(mesh, sizes=SIZES):
    fine = Mesh(mesh.devices.reshape(sizes), NAMES)
    in_specs = (P(NAMES, None), P(NAMES, None), P(("zl", "c"), None, None), P(("zl", "c"), None))
    out_specs = (P(NAMES, None), P(NAMES, None), P(NAMES))
    return jax.shard_map(
        functools.partial(body, sizes), mesh=fine, in_specs=in_specs, out_specs=out_specs, check_vma=False
    )
```

```python
import functools
import jax
import jax.numpy as jnp
import numpy as np
from jax import lax
from jax.experimental import pallas as pl
from jax.experimental.pallas import tpu as pltpu
from jax.sharding import Mesh, PartitionSpec as P

SIZES = (4, 4, 4, 2, 3, 2)
NAMES = ("zh", "x", "yh", "yl", "zl", "c")
PAD = 128


VMEM = pl.BlockSpec(memory_space=pltpu.VMEM)


def parameters(mib):
    return pltpu.CompilerParams(vmem_limit_bytes=mib * 1024 * 1024)


def quotient(values, divisor, bound):
    shift = 16
    factor = -(-(1 << shift) // divisor)
    assert all(v * factor >> shift == v // divisor for v in range(bound))
    return (values * factor) >> shift


def source_rows(sizes, core):
    _, x, yh, yl, zl, _ = sizes
    stride = {"s": 1, "zl": 4, "yl": 4 * zl, "yh": 4 * zl * yl, "x": 4 * zl * yl * yh, "zh": 4 * zl * yl * yh * x}
    bound = 8 * x * yh * yl * zl
    left = lax.broadcasted_iota(jnp.int32, (bound, 1), 0)
    source = jnp.zeros((bound, 1), jnp.int32)
    for name, size in (("zl", zl), ("yh", yh), ("zh", 2), ("yl", yl), ("x", x), ("s", 2)):
        over = quotient(left, size, bound)
        source = source + (left - over * size) * stride[name]
        left, bound = over, bound // size
    return source + 2 * jnp.where(left == 0, 1 - core, core)


def split_pairs(values):
    lane = lax.broadcasted_iota(jnp.int32, (values[0].shape[0], PAD), 1)
    parts = jnp.zeros(lane.shape, jnp.float32)
    for s, value in enumerate(values):
        high = value.astype(jnp.bfloat16).astype(jnp.float32)
        parts = jnp.where(lane == 2 * s, high, parts)
        parts = jnp.where(lane == 2 * s + 1, value - high, parts)
    return parts


def join_pairs(parts):
    lane = lax.broadcasted_iota(jnp.int32, parts.shape, 1)
    return [
        jnp.sum(jnp.where((lane == 2 * s) | (lane == 2 * s + 1), parts, 0.0), axis=1, keepdims=True)
        for s in range(2)
    ]


def term_kernel(sizes, grad_ref, ctx_ref, send_ref, keep_ref, acc):
    span = grad_ref.shape[1] // 2
    width = ctx_ref.shape[1]
    blocks, part = send_ref.shape[0], send_ref.shape[1] // 2
    column = lax.broadcasted_iota(jnp.int32, (span, span), 1)
    pick = jnp.where(source_rows(sizes, lax.axis_index("c")) == column, 1.0, 0.0).astype(jnp.bfloat16)
    ones = jnp.ones((ctx_ref.shape[0], PAD), jnp.bfloat16)
    for step in range(2):
        moved = lax.dot_general(
            pick,
            grad_ref[:, step * span : (step + 1) * span],
            (((1,), (1,)), ((), ())),
            preferred_element_type=jnp.float32,
        ).astype(jnp.bfloat16)
        acc[step, :, :width] = jnp.dot(moved, ctx_ref[...], preferred_element_type=jnp.float32)
        acc[step, :, width:] = jnp.dot(moved, ones, preferred_element_type=jnp.float32)
    for side, out in enumerate((send_ref, keep_ref)):
        for block in range(blocks):
            sums = []
            for s in range(2):
                at = ((side * 2 + s) * blocks + block) * part
                both = jnp.concatenate([acc[0, at : at + part, :], acc[1, at : at + part, :]], axis=0)
                out[block, :, s * width : (s + 1) * width] = both[:, :width].astype(jnp.bfloat16)
                sums.append(both[:, width:])
            out[block, :, 2 * width :] = split_pairs(sums).astype(jnp.bfloat16)


def local_terms(sizes, grad_out, context):
    zh, x, yh, yl, zl, _ = sizes
    width = context.shape[1]
    piece = jax.ShapeDtypeStruct((x * yl, zh * yh * zl, 2 * width + PAD), jnp.bfloat16)
    return pl.pallas_call(
        functools.partial(term_kernel, sizes),
        out_shape=(piece, piece),
        in_specs=[VMEM] * 2,
        out_specs=(VMEM, VMEM),
        scratch_shapes=[pltpu.VMEM((2, grad_out.shape[1] // 2, width + PAD), jnp.float32)],
        compiler_params=parameters(40),
        cost_estimate=pl.CostEstimate(flops=4 * 10**9, bytes_accessed=5 * 10**6, transcendentals=0),
    )(grad_out, context)


def chip_kernel(got_ref, keep_ref, out_ref):
    wide = out_ref.shape[2] - PAD
    for block in range(out_ref.shape[0]):
        total = got_ref[block].astype(jnp.float32) + keep_ref[block].astype(jnp.float32)
        out_ref[block, :, :wide] = total[:, :wide].astype(out_ref.dtype)
        out_ref[block, :, wide:] = split_pairs(join_pairs(total[:, wide:])).astype(out_ref.dtype)


def chip_sum(got, keep):
    return pl.pallas_call(
        chip_kernel,
        out_shape=jax.ShapeDtypeStruct(got.shape, got.dtype),
        in_specs=[VMEM] * 2,
        out_specs=VMEM,
        compiler_params=parameters(16),
        cost_estimate=pl.CostEstimate(flops=10**6, bytes_accessed=4 * 10**6, transcendentals=0),
    )(got, keep)


def near_kernel(got_ref, sum_ref, wide):
    chunks = got_ref.shape[2] // PAD
    wide[:, chunks:, :] = jnp.zeros((wide.shape[0], wide.shape[1] - chunks, PAD), jnp.float32)
    for chunk in range(chunks):
        lanes = slice(chunk * PAD, (chunk + 1) * PAD)
        total = got_ref[0, :, lanes].astype(jnp.float32)
        for index in range(1, got_ref.shape[0]):
            total = total + got_ref[index, :, lanes].astype(jnp.float32)
        if chunk == chunks - 1:
            total = split_pairs(join_pairs(total))
        wide[:, chunk, :] = total
    sum_ref[...] = wide[...].astype(sum_ref.dtype)


def near_sum(got):
    _, rows, lanes = got.shape
    shape = (rows, (lanes // PAD + 15) // 16 * 16, PAD)
    return pl.pallas_call(
        near_kernel,
        out_shape=jax.ShapeDtypeStruct(shape, jnp.bfloat16),
        in_specs=[VMEM],
        out_specs=VMEM,
        scratch_shapes=[pltpu.VMEM(shape, jnp.float32)],
        compiler_params=parameters(16),
        cost_estimate=pl.CostEstimate(flops=10**6, bytes_accessed=2 * 10**6, transcendentals=0),
    )(got)


def last_kernel(scale, far_ref, weight_ref, bias_ref):
    total = far_ref[0].astype(jnp.float32)
    for index in range(1, far_ref.shape[0]):
        total = total + far_ref[index].astype(jnp.float32)
    total = total * scale
    chunks = weight_ref.shape[1] // PAD
    for s in range(2):
        for chunk in range(chunks):
            at = s * chunks + chunk
            weight_ref[s : s + 1, chunk * PAD : (chunk + 1) * PAD] = total[at : at + 1, :]
    tail = total[2 * chunks : 2 * chunks + 1, :]
    lane = lax.broadcasted_iota(jnp.int32, (1, PAD), 1)
    for s in range(2):
        bias_ref[s] = jnp.sum(jnp.where((lane == 2 * s) | (lane == 2 * s + 1), tail, 0.0))


def last_sum(far, width, scale):
    return pl.pallas_call(
        functools.partial(last_kernel, scale),
        out_shape=(jax.ShapeDtypeStruct((2, width), jnp.float32), jax.ShapeDtypeStruct((2,), jnp.float32)),
        in_specs=[VMEM],
        out_specs=(pl.BlockSpec((2, width), lambda: (0, 0)), pl.BlockSpec(memory_space=pltpu.SMEM)),
        compiler_params=parameters(16),
        cost_estimate=pl.CostEstimate(flops=10**5, bytes_accessed=2 * 10**5, transcendentals=0),
    )(far)


def ctx_kernel(chips, slots, grad_ref, *refs):
    held, (*before, out_ref) = refs[: len(slots)], refs[len(slots) :]
    chip, core = lax.axis_index("zl"), lax.axis_index("c")
    rows = held[0].shape[0]
    total = before[0][...] if before else None
    for (back, other), block in zip(slots, held):
        owner = lax.rem(chip + chips - back, chips)
        side = 1 - core if other else core
        at = pl.multiple_of((2 * owner + side) * rows, rows)
        product = jnp.dot(grad_ref[:, pl.ds(at, rows)], block[...], preferred_element_type=jnp.float32)
        total = product if total is None else total + product
    out_ref[...] = total.astype(out_ref.dtype)


def ctx_product(chips, kind, grad_out, held, *before):
    tokens, depth = grad_out.shape
    steps = 2

    def rows(width):
        return pl.BlockSpec((tokens // steps, width), lambda i: (i, 0))

    blocks = list(held.values())
    width = blocks[0].shape[1]
    return pl.pallas_call(
        functools.partial(ctx_kernel, chips, tuple(held)),
        out_shape=jax.ShapeDtypeStruct((tokens, width), kind),
        grid=(steps,),
        in_specs=[rows(depth)] + [VMEM] * len(blocks) + [rows(width)] * len(before),
        out_specs=rows(width),
        compiler_params=parameters(24),
        cost_estimate=pl.CostEstimate(flops=len(blocks) * 2 * 10**8, bytes_accessed=4 * 10**6, transcendentals=0),
    )(grad_out, *blocks, *before)


def body(sizes, grad_out, context, codes, scales):
    count = int(np.prod(sizes))
    chips = sizes[4]
    ring = sizes[0] * chips
    swap = [(0, 1), (1, 0)]

    send, keep = local_terms(sizes, grad_out, context)
    got = lax.ppermute(send, "c", swap)
    block = (codes[0].astype(jnp.float32) * scales.astype(jnp.float32)).astype(jnp.bfloat16)
    held = {(0, False): block, (0, True): lax.ppermute(block, "c", swap)}
    for back in range(1, chips):
        hop = back if back <= chips // 2 else back - chips
        moves = [(i, (i + hop) % ring) for i in range(ring)]
        held[back, False] = lax.ppermute(block, ("zh", "zl"), moves)

    near = lax.all_to_all(chip_sum(got, keep), ("x", "yl"), split_axis=0, concat_axis=0, tiled=True)
    near = near_sum(near)
    _, held = lax.optimization_barrier((near, held))
    far = lax.all_to_all(near, ("zh", "yh", "zl"), split_axis=0, concat_axis=0, tiled=True)
    weight_grad, bias_grad = last_sum(far, context.shape[1], 1.0 / count)

    part = ctx_product(chips, jnp.float32, grad_out, held)
    part, held = lax.optimization_barrier((part, held))
    late = {(back, True): lax.ppermute(held[back, False], "c", swap) for back in range(1, chips)}
    ctx_grad = ctx_product(chips, jnp.bfloat16, grad_out, late, part)
    return ctx_grad, weight_grad, bias_grad


def solution(mesh, sizes=SIZES):
    fine = Mesh(mesh.devices.reshape(sizes), NAMES)
    in_specs = (P(NAMES, None), P(NAMES, None), P(("zl", "c"), None, None), P(("zl", "c"), None))
    out_specs = (P(NAMES, None), P(NAMES, None), P(NAMES))
    return jax.shard_map(
        functools.partial(body, sizes), mesh=fine, in_specs=in_specs, out_specs=out_specs, check_vma=False
    )
```
